768 devices in a mesh: dp: 96 (over x, z_hi, y), tensor: 8 (over z_lo, core).
Axes of the slice: x: 4, y: 8, z: 12 (z_hi: 3, z_lo: 4; z = z_hi * 4 + z_lo), core: 2. Of those that a mesh axis runs over, the one named last changes fastest.
Arguments:
- layer_input: bfloat16 [49152, 4608], P('dp'), may hold values from -6 to 6
- key_grad: bfloat16 [49152, 1024], P('dp', 'tensor'), may hold values from -0.25 to 0.25
- key_weight: bfloat16 [4608, 1024], P(None, 'tensor'), may hold values from -4.21875 to 4.21875
- error_state: bfloat16 [96, 4608, 1024], P('dp', None, 'tensor'), may hold values from -6 to 6
- q_start: float32 [1024, 32], P('tensor'), may hold values from -6 to 6
Outputs:
- error_next: bfloat16 [96, 4608, 1024], P('dp', None, 'tensor')
- input_grad: bfloat16 [49152, 4608], P(('dp', 'tensor'))
- p_factor: float32 [8, 4608, 32], P('tensor')
- q_factor: float32 [1024, 32], P('tensor')
The draws below stay inside these ranges and needn't reach their ends.
All inputs are finite; a program needn't handle non-finite values.
Results may differ from the reference program's by a relative error of at most 0.017.
Values may be sent and summed in bfloat16 or wider, within the bound.
A program may use at most 64 MiB of HBM per device.

```python
import jax
import jax.numpy as jnp
from jax import lax

D = 4608
KVW = 1024
R = 32
TOK_DEV = 512
TOKENS = 49152
N_DP = 96
N_TENSOR = 8


def level_of(stream_key, dims, pieces, low, high):
    gain, own = 1.0, jax.random.fold_in(stream_key, 6)
    for dim, blocks in pieces:
        heights = jnp.exp(jax.random.uniform(jax.random.fold_in(own, dim), (blocks,), jnp.float32, low / len(pieces), high / len(pieces)))
        gain = gain * jnp.repeat(heights, dims[dim] // blocks).reshape([-1 if axis == dim else 1 for axis in range(len(dims))])
    return gain


def scatter_about(own_key, dims, deviation, bound, shards=(), held_as=jnp.bfloat16):
    drawn = jax.random.normal(own_key, dims, jnp.float32) * deviation
    if len(shards) > 0:
        drawn = level_of(own_key, dims, shards, -0.22, 0.18) * drawn
    return jnp.clip(drawn, min=-bound, max=bound).astype(held_as)


def setup_inputs(seed: int = 0) -> dict:
    splits = jax.random.split(jax.random.key(seed), 6)
    return {
        "layer_input": scatter_about(splits[0], (TOKENS, D), 1.0, 6.0, ((0, 96),)),
        "key_grad": scatter_about(splits[1], (TOKENS, KVW), TOK_DEV ** -0.5, 0.25, ((0, 96), (1, 8))),
        "key_weight": scatter_about(splits[2], (D, KVW), ((TOK_DEV / KVW) ** 0.5), 4.21875, ((1, 8),)),
        "error_state": scatter_about(splits[3], (N_DP, D, KVW), 1.0, 6.0, ((0, 96), (2, 8))),
        "q_start": scatter_about(splits[4], (KVW, R), 1.0, 6.0, ((0, 8),), jnp.float32),
    }


def reference(layer_input, key_grad, key_weight, error_state, q_start):
    width = key_weight.shape[0]
    block = KVW // N_TENSOR
    total = jnp.zeros((layer_input.shape[0], width), jnp.float32)
    for head_group in range(N_TENSOR):
        grad_part = key_grad[:, head_group * block:(head_group + 1) * block]
        weight_part = key_weight[:, head_group * block:(head_group + 1) * block]
        term = jnp.dot(grad_part.astype(jnp.float32), weight_part.T.astype(jnp.float32), preferred_element_type=jnp.float32).astype(jnp.bfloat16)
        total = total + term.astype(jnp.float32)
    input_grad = total.astype(jnp.bfloat16)
    inputs_dp = layer_input.reshape(N_DP, TOK_DEV, width)
    grads_dp = key_grad.reshape(N_DP, TOK_DEV, KVW)

    def one_replica(items):
        rows, grads, errors = items
        product = jnp.einsum('td,tk->dk', rows.astype(jnp.float32), grads.astype(jnp.float32))
        return product + errors.astype(jnp.float32)
    merged = lax.map(one_replica, (inputs_dp, grads_dp, error_state))
    blocks = merged.reshape(N_DP, width, N_TENSOR, block)
    q_blocks = q_start.reshape(N_TENSOR, block, R)
    p_sum = jnp.einsum('ndtk,tkr->tdr', blocks, q_blocks, precision=lax.Precision.HIGHEST)
    gram = jnp.einsum('tdr,tds->trs', p_sum, p_sum, precision=lax.Precision.HIGHEST)
    lower = jnp.linalg.cholesky(gram)
    p_factor = lax.linalg.triangular_solve(lower, p_sum, left_side=False, lower=True, transpose_a=True)
    q_sum = jnp.einsum('ndtk,tdr->tkr', blocks, p_factor, precision=lax.Precision.HIGHEST)
    q_mean = q_sum / N_DP
    approx = jnp.einsum('tdr,tkr->dtk', p_factor, q_mean, precision=lax.Precision.HIGHEST)
    error_next = (blocks - approx[None]).reshape(N_DP, width, KVW).astype(jnp.bfloat16)
    return (error_next, input_grad, p_factor, q_mean.reshape(KVW, R))
```

```python
import functools

import jax
import jax.numpy as jnp
from jax import lax
from jax.experimental import pallas as pl
from jax.experimental.pallas import tpu as pltpu
from jax.sharding import PartitionSpec as P

MESH = pl.DeviceIdType.MESH
F32, BF16 = jnp.float32, jnp.bfloat16
NX, NZH, NY, NZL, NC = 4, 3, 8, 4, 2
D, R, KD, TOK = 4608, 32, 128, 512
XC = D // NX
HALF = 640
SL = D // 4
HIGH = lax.Precision.HIGHEST
NT = (((1,), (1,)), ((), ()))
TN = (((0,), (0,)), ((), ()))
NN = (((1,), (0,)), ((), ()))


def mm(a, b, dims, precision=None):
    return lax.dot_general(a, b, dims, precision=precision, preferred_element_type=F32)


def split(a):
    hi = a.astype(BF16)
    return hi, (a - hi.astype(F32)).astype(BF16)


def device(x, y, z, c):
    return ((x * NZH + z // NZL) * NY + y, lax.rem(z, NZL) * NC + c)


def kernel(x_hbm, g_hbm, w_hbm, e_hbm, qt_hbm,
           err_out, ig_out, pt_out, qf_out,
           xv, gv, ev, qv, wbuf, gbuf, igres, igbuf,
           ploc, ra, pa, rb, rc, pd, pe, mhi, mlo, rx, rz, ry, aug, pf, at, err,
           lsem, sa, da, sb, db, sc, dc, sd, dd, se, de,
           sx, dx, sz, dz, sy, dy, sw, dw, sg, dg, sr, dr, so, do, osem):
    dp, t = lax.axis_index("dp"), lax.axis_index("tensor")
    x, zh, y = dp // (NZH * NY), lax.rem(dp // NY, NZH), lax.rem(dp, NY)
    zl, c = t // NC, lax.rem(t, NC)
    z = zh * NZL + zl
    oc = 1 - c
    yb = lax.rem(y, 2)
    yp = y + 1 - 2 * yb

    def zdev(k, core):
        return device(x, y, lax.rem(z + k + 12, 12), core)

    def xdev(k):
        return device(lax.rem(x + k, NX), y, z, c)

    def ydev(k):
        return device(x, lax.rem(y + k, NY), z, c)

    def gdev(k):
        return device(x, y, zh * NZL + lax.rem(zl + k, NZL), c)

    other, part, partother = device(x, y, z, oc), device(x, yp, z, c), device(x, yp, z, oc)

    def remote(src, dst, ssem, rsem, dev):
        return pltpu.make_async_remote_copy(src, dst, ssem, rsem, device_id=dev, device_id_type=MESH)

    loads = [pltpu.make_async_copy(g_hbm, gv, lsem.at[0]), pltpu.make_async_copy(qt_hbm, qv, lsem.at[1]),
             pltpu.make_async_copy(e_hbm, ev, lsem.at[2])]
    for l in loads:
        l.start()

    def xload(k):
        cols = pl.ds(pl.multiple_of(lax.rem(x + k, NX) * XC, 128), XC)
        return pltpu.make_async_copy(x_hbm.at[:, cols], xv.at[:, cols], lsem.at[3 + k % 4])
    for k in (1, 2, 3, 4):
        xload(k).start()
    wcol = pl.multiple_of((c * NZL + zl) * KD, KD)
    wrow = lambda core, off=0: pl.multiple_of((yb * 2 + core) * SL + off, 64)
    wown = pltpu.make_async_copy(w_hbm.at[pl.ds(wrow(c), SL)], wbuf.at[:, pl.ds(wcol, KD)], lsem.at[7])
    wown.start()

    barrier = pltpu.get_barrier_semaphore()
    greet = ([xdev(k) for k in (1, 2, 3)] + [ydev(k) for k in range(1, 8)] + [zdev(k, c) for k in (4, -4)]
             + [gdev(k) for k in (1, 2, 3)] + [zdev(k, cc) for k in (1, -1, 2, -2) for cc in (0, 1)] + [other, partother])
    for d in greet:
        pl.semaphore_signal(barrier, inc=1, device_id=d, device_id_type=MESH)

    loads[0].wait()
    loads[1].wait()
    qh, ql = split(qv[...])
    q2 = jnp.concatenate([qh, ql], axis=0)
    gq = mm(q2, gv[...], NT)
    gh, gl = split(gq[:R] + gq[R:])
    g2 = jnp.concatenate([gh, gl], axis=0)

    pl.semaphore_wait(barrier, len(greet))

    gsend = [remote(gv.at[pl.ds(pl.multiple_of(lax.rem(zl + k, NZL) * 128, 128), 128)], gbuf.at[0, :, pl.ds(wcol, KD)],
                    sg.at[k - 1], dg.at[k - 1], gdev(k)) for k in (1, 2, 3)]
    for s in gsend:
        s.start()
    gbuf[0, :, pl.ds(wcol, KD)] = gv[pl.ds(pl.multiple_of(zl * 128, 128), 128)]
    loads[2].wait()

    asend = []
    for k in (2, 1, 3, 4):
        xload(k).wait()
        ch = lax.rem(x + k, NX)
        base = pl.multiple_of(ch * XC, 128)
        for off in (0, 384, 768):
            r = mm(g2, xv[:, pl.ds(base + off, 384)], NN) + mm(q2, ev[pl.ds(base + off, 384)], NT)
            ploc[ch, :, pl.ds(off, 384)] = r[:R] + r[R:]
        if k < 4:
            a = remote(ploc.at[ch], ra.at[k - 1], sa.at[k - 1], da.at[k - 1], xdev(k))
            a.start()
            asend.append(a)

    wsend = [remote(w_hbm.at[pl.ds(wrow(oc), SL)], wbuf.at[:, pl.ds(wcol, KD)], sw.at[0], dw.at[0], other)]
    i = 1
    for k in (1, -1):
        for cc in (0, 1):
            rel = (cc + c) - 2 * cc * c
            wsend.append(remote(w_hbm.at[pl.ds(wrow(cc), SL)], wbuf.at[:, pl.ds(wcol, KD)],
                                sw.at[i], dw.at[(1 if k == 1 else 3) + rel], zdev(k, cc)))
            i += 1
    for k in (2, -2):
        off = 0 if k == 2 else SL // 2
        for cc in (0, 1):
            rel = (cc + c) - 2 * cc * c
            wsend.append(remote(w_hbm.at[pl.ds(wrow(cc, off), SL // 2)], wbuf.at[pl.ds(off, SL // 2), pl.ds(wcol, KD)],
                                sw.at[i], dw.at[(5 if k == 2 else 7) + rel], zdev(k, cc)))
            i += 1
    for s in wsend:
        s.start()

    def merge(j, carry):
        rows = pl.ds(pl.multiple_of(j * 256, 256), 256)
        m = mm(xv[:, rows], gv[...], TN) + ev[rows].astype(F32)
        h, l = split(m)
        mhi[rows] = h
        mlo[rows] = l
        return carry
    lax.fori_loop(0, 18, merge, 0)

    for s in asend:
        s.wait_recv()
    tot = ploc[x] + ra[0] + ra[1] + ra[2]
    pa[0] = tot[:, :HALF]
    pa[1, :, pl.ds(0, XC - HALF)] = tot[:, HALF:]
    pa[1, :, pl.ds(XC - HALF, 2 * HALF - XC)] = jnp.zeros((R, 2 * HALF - XC), F32)

    def piece(ref, j):
        return ref.at[j // 4, pl.ds(pl.multiple_of(lax.rem(j, 4) * 8, 8), 8)]

    bsend = []
    for k in range(1, 8):
        b = remote(piece(pa, lax.rem(y + k, NY)), rb.at[k - 1], sb.at[k - 1], db.at[k - 1], ydev(k))
        b.start()
        bsend.append(b)

    for s in gsend:
        s.wait_recv()
    half = pl.ds(pl.multiple_of(c * 512, 512), 512)
    rsend = [remote(gbuf.at[0, :, half], gbuf.at[i, :, half], sr.at[k], dr.at[k], d)
             for k, (i, d) in enumerate([(0, other), (1, part), (1, partother)])]
    for s in rsend:
        s.start()

    for s in bsend:
        s.wait_recv()
    own = piece(pa, y)[...]
    for k in range(7):
        own = own + rb[k]
    rc[zh] = own

    csend = []
    for k, dz_ in ((0, 4), (1, -4)):
        b = remote(rc.at[zh], rc.at[zh], sc.at[k], dc.at[k], zdev(dz_, c))
        b.start()
        csend.append(b)
    for s in csend:
        s.wait_recv()
    piece(pd, y)[...] = rc[0] + rc[1] + rc[2]

    dsend = []
    for k in range(1, 8):
        b = remote(piece(pd, y), piece(pd, y), sd.at[k - 1], dd.at[k - 1], ydev(k))
        b.start()
        dsend.append(b)
    for s in dsend:
        s.wait_recv()

    pe[x] = pd[...]
    esend = []
    for k in (2, 1, 3):
        b = remote(pd, pe.at[x], se.at[k - 1], de.at[k - 1], xdev(k))
        b.start()
        esend.append(b)

    def right(ch):
        tot = jnp.zeros((R, KD), F32)
        for h, n in ((0, HALF), (1, XC - HALF)):
            ph, pl_ = split(pe[ch, h, :, :n])
            rows = pl.ds(pl.multiple_of(ch * XC + h * HALF, 128), n)
            r = mm(jnp.concatenate([ph, pl_], axis=0), mhi[rows], NN)
            tot = tot + r[:R] + r[R:] + mm(ph, mlo[rows], NN)
        return tot

    qp = right(x)
    for k, s in ((1, esend[1]), (3, esend[2]), (2, esend[0])):
        s.wait_recv()
        qp = qp + right(lax.rem(x + 4 - k, NX))

    rx[x] = qp
    fsend = []
    for k in (1, 2, 3):
        b = remote(rx.at[x], rx.at[x], sx.at[k - 1], dx.at[k - 1], xdev(k))
        b.start()
        fsend.append(b)

    gram = jnp.zeros((R, R), F32)
    for ch in range(NX):
        for h, n in ((0, HALF), (1, XC - HALF)):
            b = pe[ch, h, :, :n]
            gram = gram + mm(b, b, NT, HIGH)
    row = lax.broadcasted_iota(jnp.int32, (R, KD), 0)
    col = lax.broadcasted_iota(jnp.int32, (R, KD), 1)
    aug[...] = jnp.where(col == row + R, 1.0, 0.0)
    aug[:, :R] = gram

    def factor(k, carry):
        a = aug[...]
        r = jnp.sum(jnp.where(row == k, a, 0.0), axis=0, keepdims=True)
        cl = jnp.sum(jnp.where(col == k, a, 0.0), axis=1, keepdims=True)
        pivot = jnp.sum(jnp.where(col[:1] == k, r, 0.0), axis=1, keepdims=True)
        s = 1.0 / jnp.sqrt(pivot)
        rn = r * s
        aug[...] = jnp.where(row == k, rn, jnp.where(row > k, a - (cl * s) * rn, a))
        return carry

    for s in fsend:
        s.wait_recv()
    rz[zh] = rx[0] + rx[1] + rx[2] + rx[3]

    hsend = []
    for k, dz_ in ((0, 4), (1, -4)):
        b = remote(rz.at[zh], rz.at[zh], sz.at[k], dz.at[k], zdev(dz_, c))
        b.start()
        hsend.append(b)
    lax.fori_loop(0, 16, factor, 0)
    for s in hsend:
        s.wait_recv()
    ry[y] = rz[0] + rz[1] + rz[2]

    ysend = []
    for k in range(1, 8):
        b = remote(ry.at[y], ry.at[y], sy.at[k - 1], dy.at[k - 1], ydev(k))
        b.start()
        ysend.append(b)
    lax.fori_loop(16, R, factor, 0)
    linv = aug[:, R:2 * R]
    for ch in range(NX):
        for h, n in ((0, HALF), (1, XC - HALF)):
            cols = pl.ds(ch * XC + h * HALF, n)
            p = mm(linv, pe[ch, h, :, :n], NN, HIGH)
            pf[:, cols] = p
            ph, pl_ = split(p)
            at[pl.ds(0, R), cols] = ph
            at[pl.ds(R, R), cols] = pl_
            at[pl.ds(2 * R, R), cols] = ph
    at[pl.ds(3 * R, R)] = jnp.zeros((R, D), BF16)
    pout = pltpu.make_async_copy(pf, pt_out, osem.at[0])
    pout.start()
    for s in ysend:
        s.wait_recv()
    q = ry[0]
    for k in range(1, 8):
        q = q + ry[k]
    qf = mm(linv, q, NN, HIGH) * (1.0 / (NX * NY * NZH))
    qf_out[...] = qf
    bh, bl = split(qf)
    b4 = jnp.concatenate([bh, bh, bl, jnp.zeros_like(bl)], axis=0)

    def finish(j, carry):
        rows = pl.ds(pl.multiple_of(j * 256, 256), 256)
        a = mm(at[:, rows], b4, TN)
        err[rows] = ((mhi[rows].astype(F32) - a) + mlo[rows].astype(F32)).astype(BF16)
        return carry
    lax.fori_loop(0, 18, finish, 0)
    eout = pltpu.make_async_copy(err, err_out, osem.at[1])
    eout.start()

    for s in rsend:
        s.wait_recv()
    wown.wait()
    for s in wsend:
        s.wait_recv()

    def grad(j, carry):
        rows = pl.ds(pl.multiple_of(j * 384, 128), 384)
        for b in range(2):
            igres[pl.ds(b * 128, 128), rows] = mm(gbuf[b], wbuf[rows], NT).astype(BF16)
        return carry
    lax.fori_loop(0, 3, grad, 0)
    scol = pl.ds(pl.multiple_of((yb * 2 + c) * SL, 128), SL)
    osend = []
    for k, (b, core, d) in enumerate([(0, oc, other), (1, c, part), (1, oc, partother)]):
        s = remote(igres.at[pl.ds(pl.multiple_of(b * 128 + core * 64, 64), 64)], igbuf.at[:, scol], so.at[k], do.at[k], d)
        s.start()
        osend.append(s)
    igbuf[:, scol] = igres[pl.ds(pl.multiple_of(c * 64, 64), 64)]
    for s in osend:
        s.wait_recv()
    iout = pltpu.make_async_copy(igbuf, ig_out, osem.at[2])
    iout.start()
    for s in asend + bsend + csend + dsend + esend + fsend + hsend + ysend + wsend + gsend + rsend + osend:
        s.wait_send()
    pout.wait()
    eout.wait()
    iout.wait()


def shards(layer_input, key_grad, key_weight, error_state, q_start):
    dma = lambda n: pltpu.SemaphoreType.DMA((n,))
    any_ = pl.BlockSpec(memory_space=pl.ANY)
    err, ig, pt, qt = pl.pallas_call(
        kernel,
        out_shape=(
            jax.ShapeDtypeStruct((D, KD), BF16),
            jax.ShapeDtypeStruct((TOK // 8, D), BF16),
            jax.ShapeDtypeStruct((R, D), F32),
            jax.ShapeDtypeStruct((R, KD), F32),
        ),
        in_specs=[any_] * 5,
        out_specs=(any_, any_, any_, pl.BlockSpec(memory_space=pltpu.VMEM)),
        scratch_shapes=[
            pltpu.VMEM((TOK, D), BF16), pltpu.VMEM((TOK, KD), BF16), pltpu.VMEM((D, KD), BF16), pltpu.VMEM((R, KD), F32),
            pltpu.VMEM((SL, 1024), BF16), pltpu.VMEM((2, 128, 1024), BF16), pltpu.VMEM((256, SL), BF16), pltpu.VMEM((64, D), BF16),
            pltpu.VMEM((NX, R, XC), F32), pltpu.VMEM((3, R, XC), F32), pltpu.VMEM((2, R, HALF), F32),
            pltpu.VMEM((7, 8, HALF), F32), pltpu.VMEM((NZH, 8, HALF), F32), pltpu.VMEM((2, R, HALF), F32),
            pltpu.VMEM((NX, 2, R, HALF), F32), pltpu.VMEM((D, KD), BF16), pltpu.VMEM((D, KD), BF16),
            pltpu.VMEM((NX, R, KD), F32), pltpu.VMEM((NZH, R, KD), F32), pltpu.VMEM((NY, R, KD), F32),
            pltpu.VMEM((R, KD), F32), pltpu.VMEM((R, D), F32), pltpu.VMEM((KD, D), BF16), pltpu.VMEM((D, KD), BF16),
            dma(8), dma(3), dma(3), dma(7), dma(7), dma(2), dma(2), dma(7), dma(7), dma(3), dma(3),
            dma(3), dma(3), dma(2), dma(2), dma(7), dma(7), dma(9), dma(9), dma(3), dma(3), dma(3), dma(3), dma(3), dma(3), dma(3),
        ],
        compiler_params=pltpu.CompilerParams(collective_id=0, has_side_effects=True, vmem_limit_bytes=48 << 20),
        name="powersgd",
    )(layer_input, key_grad, key_weight, error_state[0], q_start.T)
    return (err[None], ig, pt.T[None], qt.T)


def solution(mesh):
    return jax.shard_map(
        shards,
        mesh=mesh,
        in_specs=(
            P("dp", None),
            P("dp", "tensor"),
            P(None, "tensor"),
            P("dp", None, "tensor"),
            P("tensor", None),
        ),
        out_specs=(
            P("dp", None, "tensor"),
            P(("dp", "tensor"), None),
            P("tensor", None, None),
            P("tensor", None),
        ),
        check_vma=False,
    )
```

```python
import functools

import jax
import jax.numpy as jnp
from jax import lax
from jax.experimental import pallas as pl
from jax.experimental.pallas import tpu as pltpu
from jax.sharding import PartitionSpec as P

MESH = pl.DeviceIdType.MESH
F32, BF16 = jnp.float32, jnp.bfloat16
NX, NZH, NY, NZL, NC = 4, 3, 8, 4, 2
D, R, KD, TOK = 4608, 32, 128, 512
XC = D // NX
HALF = 640
SL = D // 4
HIGH = lax.Precision.HIGHEST
NT = (((1,), (1,)), ((), ()))
TN = (((0,), (0,)), ((), ()))
NN = (((1,), (0,)), ((), ()))


def mm(a, b, dims, precision=None):
    return lax.dot_general(a, b, dims, precision=precision, preferred_element_type=F32)


def split(a):
    hi = a.astype(BF16)
    return hi, (a - hi.astype(F32)).astype(BF16)


def device(x, y, z, c):
    return ((x * NZH + z // NZL) * NY + y, lax.rem(z, NZL) * NC + c)


def kernel(x_hbm, g_hbm, w_hbm, e_hbm, qt_hbm,
           at_out, mhi_out, mlo_out, ig_out, pf_out, qf_out,
           xv, gv, ev, qv, wbuf, gbuf, igres, igbuf,
           ploc, ra, pa, rb, rc, pd, pe, mhi, mlo, rx, rz, ry, aug, pf, at, qf,
           lsem, sa, da, sb, db, sc, dc, sd, dd, se, de,
           sx, dx, sz, dz, sy, dy, sw, dw, sg, dg, sr, dr, so, do, osem):
    dp, t = lax.axis_index("dp"), lax.axis_index("tensor")
    x, zh, y = dp // (NZH * NY), lax.rem(dp // NY, NZH), lax.rem(dp, NY)
    zl, c = t // NC, lax.rem(t, NC)
    z = zh * NZL + zl
    oc = 1 - c
    yb = lax.rem(y, 2)
    yp = y + 1 - 2 * yb

    def zdev(k, core):
        return device(x, y, lax.rem(z + k + 12, 12), core)

    def xdev(k):
        return device(lax.rem(x + k, NX), y, z, c)

    def ydev(k):
        return device(x, lax.rem(y + k, NY), z, c)

    def gdev(k):
        return device(x, y, zh * NZL + lax.rem(zl + k, NZL), c)

    other, part, partother = device(x, y, z, oc), device(x, yp, z, c), device(x, yp, z, oc)

    def remote(src, dst, ssem, rsem, dev):
        return pltpu.make_async_remote_copy(src, dst, ssem, rsem, device_id=dev, device_id_type=MESH)

    loads = [pltpu.make_async_copy(g_hbm, gv, lsem.at[0]), pltpu.make_async_copy(qt_hbm, qv, lsem.at[1]),
             pltpu.make_async_copy(e_hbm, ev, lsem.at[2])]
    for l in loads:
        l.start()

    def xload(k):
        cols = pl.ds(pl.multiple_of(lax.rem(x + k, NX) * XC, 128), XC)
        return pltpu.make_async_copy(x_hbm.at[:, cols], xv.at[:, cols], lsem.at[3 + k % 4])
    for k in (1, 2, 3, 4):
        xload(k).start()
    wcol = pl.multiple_of((c * NZL + zl) * KD, KD)
    wrow = lambda core, off=0: pl.multiple_of((yb * 2 + core) * SL + off, 64)
    wown = pltpu.make_async_copy(w_hbm.at[pl.ds(wrow(c), SL)], wbuf.at[:, pl.ds(wcol, KD)], lsem.at[7])
    wown.start()

    barrier = pltpu.get_barrier_semaphore()
    greet = ([xdev(k) for k in (1, 2, 3)] + [ydev(k) for k in range(1, 8)] + [zdev(k, c) for k in (4, -4)]
             + [gdev(k) for k in (1, 2, 3)] + [zdev(k, cc) for k in (1, -1, 2, -2) for cc in (0, 1)] + [other, partother])
    for d in greet:
        pl.semaphore_signal(barrier, inc=1, device_id=d, device_id_type=MESH)

    loads[0].wait()
    loads[1].wait()
    qh, ql = split(qv[...])
    q2 = jnp.concatenate([qh, ql], axis=0)
    gq = mm(q2, gv[...], NT)
    gh, gl = split(gq[:R] + gq[R:])
    g2 = jnp.concatenate([gh, gl], axis=0)

    pl.semaphore_wait(barrier, len(greet))

    gsend = [remote(gv.at[pl.ds(pl.multiple_of(lax.rem(zl + k, NZL) * 128, 128), 128)], gbuf.at[0, :, pl.ds(wcol, KD)],
                    sg.at[k - 1], dg.at[k - 1], gdev(k)) for k in (1, 2, 3)]
    for s in gsend:
        s.start()
    gbuf[0, :, pl.ds(wcol, KD)] = gv[pl.ds(pl.multiple_of(zl * 128, 128), 128)]
    loads[2].wait()

    asend = []
    for k in (2, 1, 3, 4):
        xload(k).wait()
        ch = lax.rem(x + k, NX)
        base = pl.multiple_of(ch * XC, 128)
        for off in (0, 384, 768):
            r = mm(g2, xv[:, pl.ds(base + off, 384)], NN) + mm(q2, ev[pl.ds(base + off, 384)], NT)
            ploc[ch, :, pl.ds(off, 384)] = r[:R] + r[R:]
        if k < 4:
            a = remote(ploc.at[ch], ra.at[k - 1], sa.at[k - 1], da.at[k - 1], xdev(k))
            a.start()
            asend.append(a)

    wsend = [remote(w_hbm.at[pl.ds(wrow(oc), SL)], wbuf.at[:, pl.ds(wcol, KD)], sw.at[0], dw.at[0], other)]
    i = 1
    for k in (1, -1):
        for cc in (0, 1):
            rel = (cc + c) - 2 * cc * c
            wsend.append(remote(w_hbm.at[pl.ds(wrow(cc), SL)], wbuf.at[:, pl.ds(wcol, KD)],
                                sw.at[i], dw.at[(1 if k == 1 else 3) + rel], zdev(k, cc)))
            i += 1
    for k in (2, -2):
        off = 0 if k == 2 else SL // 2
        for cc in (0, 1):
            rel = (cc + c) - 2 * cc * c
            wsend.append(remote(w_hbm.at[pl.ds(wrow(cc, off), SL // 2)], wbuf.at[pl.ds(off, SL // 2), pl.ds(wcol, KD)],
                                sw.at[i], dw.at[(5 if k == 2 else 7) + rel], zdev(k, cc)))
            i += 1
    for s in wsend:
        s.start()

    def merge(j, carry):
        rows = pl.ds(pl.multiple_of(j * 256, 256), 256)
        m = mm(xv[:, rows], gv[...], TN) + ev[rows].astype(F32)
        h, l = split(m)
        mhi[rows] = h
        mlo[rows] = l
        return carry
    lax.fori_loop(0, 18, merge, 0)
    outs = []

    def put(src, dst):
        cp = pltpu.make_async_copy(src, dst, osem.at[len(outs)])
        cp.start()
        outs.append(cp)
    put(mhi, mhi_out)
    put(mlo, mlo_out)

    for s in asend:
        s.wait_recv()
    tot = ploc[x] + ra[0] + ra[1] + ra[2]
    pa[0] = tot[:, :HALF]
    pa[1, :, pl.ds(0, XC - HALF)] = tot[:, HALF:]
    pa[1, :, pl.ds(XC - HALF, 2 * HALF - XC)] = jnp.zeros((R, 2 * HALF - XC), F32)

    def piece(ref, j):
        return ref.at[j // 4, pl.ds(pl.multiple_of(lax.rem(j, 4) * 8, 8), 8)]

    bsend = []
    for k in range(1, 8):
        b = remote(piece(pa, lax.rem(y + k, NY)), rb.at[k - 1], sb.at[k - 1], db.at[k - 1], ydev(k))
        b.start()
        bsend.append(b)

    for s in gsend:
        s.wait_recv()
    half = pl.ds(pl.multiple_of(c * 512, 512), 512)
    rsend = [remote(gbuf.at[0, :, half], gbuf.at[i, :, half], sr.at[k], dr.at[k], d)
             for k, (i, d) in enumerate([(0, other), (1, part), (1, partother)])]
    for s in rsend:
        s.start()

    for s in bsend:
        s.wait_recv()
    own = piece(pa, y)[...]
    for k in range(7):
        own = own + rb[k]
    rc[zh] = own

    csend = []
    for k, dz_ in ((0, 4), (1, -4)):
        b = remote(rc.at[zh], rc.at[zh], sc.at[k], dc.at[k], zdev(dz_, c))
        b.start()
        csend.append(b)
    for s in csend:
        s.wait_recv()
    piece(pd, y)[...] = rc[0] + rc[1] + rc[2]

    dsend = []
    for k in range(1, 8):
        b = remote(piece(pd, y), piece(pd, y), sd.at[k - 1], dd.at[k - 1], ydev(k))
        b.start()
        dsend.append(b)
    for s in dsend:
        s.wait_recv()

    pe[x] = pd[...]
    esend = []
    for k in (2, 1, 3):
        b = remote(pd, pe.at[x], se.at[k - 1], de.at[k - 1], xdev(k))
        b.start()
        esend.append(b)

    for s in rsend:
        s.wait_recv()
    wown.wait()
    for s in wsend:
        s.wait_recv()

    def grad(j, carry):
        rows = pl.ds(pl.multiple_of(j * 384, 128), 384)
        for b in range(2):
            igres[pl.ds(b * 128, 128), rows] = mm(gbuf[b], wbuf[rows], NT).astype(BF16)
        return carry
    lax.fori_loop(0, 3, grad, 0)
    scol = pl.ds(pl.multiple_of((yb * 2 + c) * SL, 128), SL)
    osend = []
    for k, (b, core, d) in enumerate([(0, oc, other), (1, c, part), (1, oc, partother)]):
        s = remote(igres.at[pl.ds(pl.multiple_of(b * 128 + core * 64, 64), 64)], igbuf.at[:, scol], so.at[k], do.at[k], d)
        s.start()
        osend.append(s)
    igbuf[:, scol] = igres[pl.ds(pl.multiple_of(c * 64, 64), 64)]
    def right(ch):
        tot = jnp.zeros((R, KD), F32)
        for h, n in ((0, HALF), (1, XC - HALF)):
            ph, pl_ = split(pe[ch, h, :, :n])
            rows = pl.ds(pl.multiple_of(ch * XC + h * HALF, 128), n)
            r = mm(jnp.concatenate([ph, pl_], axis=0), mhi[rows], NN)
            tot = tot + r[:R] + r[R:] + mm(ph, mlo[rows], NN)
        return tot

    qp = right(x)
    for k, s in ((1, esend[1]), (3, esend[2]), (2, esend[0])):
        s.wait_recv()
        qp = qp + right(lax.rem(x + 4 - k, NX))

    rx[x] = qp
    fsend = []
    for k in (1, 2, 3):
        b = remote(rx.at[x], rx.at[x], sx.at[k - 1], dx.at[k - 1], xdev(k))
        b.start()
        fsend.append(b)

    gram = jnp.zeros((R, R), F32)
    for ch in range(NX):
        for h, n in ((0, HALF), (1, XC - HALF)):
            b = pe[ch, h, :, :n]
            gram = gram + mm(b, b, NT, HIGH)
    row = lax.broadcasted_iota(jnp.int32, (R, KD), 0)
    col = lax.broadcasted_iota(jnp.int32, (R, KD), 1)
    aug[...] = jnp.where(col == row + R, 1.0, 0.0)
    aug[:, :R] = gram

    def factor(k, carry):
        a = aug[...]
        r = jnp.sum(jnp.where(row == k, a, 0.0), axis=0, keepdims=True)
        cl = jnp.sum(jnp.where(col == k, a, 0.0), axis=1, keepdims=True)
        pivot = jnp.sum(jnp.where(col[:1] == k, r, 0.0), axis=1, keepdims=True)
        s = 1.0 / jnp.sqrt(pivot)
        rn = r * s
        aug[...] = jnp.where(row == k, rn, jnp.where(row > k, a - (cl * s) * rn, a))
        return carry

    for s in fsend:
        s.wait_recv()
    rz[zh] = rx[0] + rx[1] + rx[2] + rx[3]

    hsend = []
    for k, dz_ in ((0, 4), (1, -4)):
        b = remote(rz.at[zh], rz.at[zh], sz.at[k], dz.at[k], zdev(dz_, c))
        b.start()
        hsend.append(b)
    lax.fori_loop(0, 16, factor, 0)
    for s in hsend:
        s.wait_recv()
    ry[y] = rz[0] + rz[1] + rz[2]

    ysend = []
    for k in range(1, 8):
        b = remote(ry.at[y], ry.at[y], sy.at[k - 1], dy.at[k - 1], ydev(k))
        b.start()
        ysend.append(b)
    lax.fori_loop(16, R, factor, 0)
    linv = aug[:, R:2 * R]
    for ch in range(NX):
        for h, n in ((0, HALF), (1, XC - HALF)):
            cols = pl.ds(ch * XC + h * HALF, n)
            p = mm(linv, pe[ch, h, :, :n], NN, HIGH)
            pf[:, cols] = p
            ph, pl_ = split(p)
            at[pl.ds(0, R), cols] = ph
            at[pl.ds(R, R), cols] = pl_
            at[pl.ds(2 * R, R), cols] = ph
    at[pl.ds(3 * R, R)] = jnp.zeros((R, D), BF16)
    put(at, at_out)
    put(pf, pf_out)
    for s in osend:
        s.wait_recv()
    put(igbuf, ig_out)
    for s in ysend:
        s.wait_recv()
    q = ry[0]
    for k in range(1, 8):
        q = q + ry[k]
    qf[...] = mm(linv, q, NN, HIGH) * (1.0 / (NX * NY * NZH))
    put(qf, qf_out)
    for s in asend + bsend + csend + dsend + esend + fsend + hsend + ysend + wsend + gsend + rsend + osend:
        s.wait_send()
    for s in outs:
        s.wait()


def last(at_in, mhi_in, mlo_in, ig_in, pf_in, qf_in, err_out, ig_out, pt_out, qf_out, at, mhi, mlo, qf, ig, pf, err, sem, lsem):
    def load(a, b, i):
        cp = pltpu.make_async_copy(a, b, lsem.at[i])
        cp.start()
        return cp
    qload = load(qf_in, qf, 0)
    loads = []
    for h in range(3):
        part = pl.ds(h * 1536, 1536)
        loads.append([load(at_in.at[:, part], at.at[:, part], 1 + 3 * h), load(mhi_in.at[part], mhi.at[part], 2 + 3 * h),
                      load(mlo_in.at[part], mlo.at[part], 3 + 3 * h)])
    through = [(qload, qf, qf_out), (load(ig_in, ig, 10), ig, ig_out), (load(pf_in, pf, 11), pf, pt_out)]
    copies = [pltpu.make_async_copy(b, o, sem.at[i]) for i, (l, b, o) in enumerate(through)]
    qload.wait()
    copies[0].start()
    bh, bl = split(qf[...])
    b4 = jnp.concatenate([bh, bh, bl, jnp.zeros_like(bl)], axis=0)
    for h in range(3):
        for l in loads[h]:
            l.wait()

        def finish(j, carry):
            rows = pl.ds(pl.multiple_of(h * 1536 + j * 256, 256), 256)
            a = mm(at[:, rows], b4, TN)
            err[rows] = ((mhi[rows].astype(F32) - a) + mlo[rows].astype(F32)).astype(BF16)
            return carry
        lax.fori_loop(0, 6, finish, 0)
        part = pl.ds(h * 1536, 1536)
        c = pltpu.make_async_copy(err.at[part], err_out.at[part], sem.at[3 + h])
        c.start()
        copies.append(c)
        if h < 2:
            through[1 + h][0].wait()
            copies[1 + h].start()
    for c in copies:
        c.wait()


def shards(layer_input, key_grad, key_weight, error_state, q_start):
    dma = lambda n: pltpu.SemaphoreType.DMA((n,))
    hbm = pl.BlockSpec(memory_space=pltpu.HBM)
    shape = jax.ShapeDtypeStruct
    parts = pl.pallas_call(
        kernel,
        out_shape=(shape((KD, D), BF16), shape((D, KD), BF16), shape((D, KD), BF16),
                   shape((TOK // 8, D), BF16), shape((R, D), F32), shape((R, KD), F32)),
        in_specs=[hbm] * 5,
        out_specs=[hbm] * 6,
        scratch_shapes=[
            pltpu.VMEM((TOK, D), BF16), pltpu.VMEM((TOK, KD), BF16), pltpu.VMEM((D, KD), BF16), pltpu.VMEM((R, KD), F32),
            pltpu.VMEM((SL, 1024), BF16), pltpu.VMEM((2, 128, 1024), BF16), pltpu.VMEM((256, SL), BF16), pltpu.VMEM((64, D), BF16),
            pltpu.VMEM((NX, R, XC), F32), pltpu.VMEM((3, R, XC), F32), pltpu.VMEM((2, R, HALF), F32),
            pltpu.VMEM((7, 8, HALF), F32), pltpu.VMEM((NZH, 8, HALF), F32), pltpu.VMEM((2, R, HALF), F32),
            pltpu.VMEM((NX, 2, R, HALF), F32), pltpu.VMEM((D, KD), BF16), pltpu.VMEM((D, KD), BF16),
            pltpu.VMEM((NX, R, KD), F32), pltpu.VMEM((NZH, R, KD), F32), pltpu.VMEM((NY, R, KD), F32),
            pltpu.VMEM((R, KD), F32), pltpu.VMEM((R, D), F32), pltpu.VMEM((KD, D), BF16), pltpu.VMEM((R, KD), F32),
            dma(8), dma(3), dma(3), dma(7), dma(7), dma(2), dma(2), dma(7), dma(7), dma(3), dma(3),
            dma(3), dma(3), dma(2), dma(2), dma(7), dma(7), dma(9), dma(9), dma(3), dma(3), dma(3), dma(3), dma(3), dma(3), dma(6),
        ],
        compiler_params=pltpu.CompilerParams(collective_id=0, has_side_effects=True, vmem_limit_bytes=60 << 20),
        name="powersgd",
    )(layer_input, key_grad, key_weight, error_state[0], q_start.T)
    err, ig, pt, qt = pl.pallas_call(
        last,
        out_shape=(shape((D, KD), BF16), shape((TOK // 8, D), BF16), shape((R, D), F32), shape((R, KD), F32)),
        in_specs=[hbm] * 6,
        out_specs=[hbm] * 4,
        scratch_shapes=[pltpu.VMEM((KD, D), BF16), pltpu.VMEM((D, KD), BF16), pltpu.VMEM((D, KD), BF16), pltpu.VMEM((R, KD), F32),
                        pltpu.VMEM((64, D), BF16), pltpu.VMEM((R, D), F32), pltpu.VMEM((D, KD), BF16), dma(6), dma(12)],
        compiler_params=pltpu.CompilerParams(vmem_limit_bytes=60 << 20),
        name="finish",
    )(*parts)
    return (err[None], ig, pt.T[None], qt.T)


def solution(mesh):
    return jax.shard_map(
        shards,
        mesh=mesh,
        in_specs=(
            P("dp", None),
            P("dp", "tensor"),
            P(None, "tensor"),
            P("dp", None, "tensor"),
            P("tensor", None),
        ),
        out_specs=(
            P("dp", None, "tensor"),
            P(("dp", "tensor"), None),
            P("tensor", None, None),
            P("tensor", None),
        ),
        check_vma=False,
    )
```

```python
import functools

import jax
import jax.numpy as jnp
from jax import lax
from jax.experimental import pallas as pl
from jax.experimental.pallas import tpu as pltpu
from jax.sharding import PartitionSpec as P

MESH = pl.DeviceIdType.MESH
F32, BF16 = jnp.float32, jnp.bfloat16
NX, NZH, NY, NZL, NC = 4, 3, 8, 4, 2
D, R, KD, TOK = 4608, 32, 128, 512
XC = D // NX
HALF = 640
SL = D // 4
HIGH = lax.Precision.HIGHEST
NT = (((1,), (1,)), ((), ()))
TN = (((0,), (0,)), ((), ()))
NN = (((1,), (0,)), ((), ()))


def mm(a, b, dims, precision=None):
    return lax.dot_general(a, b, dims, precision=precision, preferred_element_type=F32)


def split(a):
    hi = a.astype(BF16)
    return hi, (a - hi.astype(F32)).astype(BF16)


def device(x, y, z, c):
    return ((x * NZH + z // NZL) * NY + y, lax.rem(z, NZL) * NC + c)


def kernel(x_hbm, g_hbm, w_hbm, e_hbm, qt_hbm,
           at_out, mhi_out, mlo_out, ig_out, pf_out, qf_out,
           xv, gv, ev, qv, wbuf, gbuf, igres, igbuf,
           ploc, pown, ra, pa, rb, rc, pd, pb, pe, mhi, mlo, rx, rz, ry, aug, pf, at, qf,
           lsem, sa, da, sb, db, sc, dc, sd, dd, se, de,
           sx, dx, sz, dz, sy, dy, sw, dw, sg, dg, sr, dr, so, do, osem):
    dp, t = lax.axis_index("dp"), lax.axis_index("tensor")
    x, zh, y = dp // (NZH * NY), lax.rem(dp // NY, NZH), lax.rem(dp, NY)
    zl, c = t // NC, lax.rem(t, NC)
    z = zh * NZL + zl
    oc = 1 - c
    yb = lax.rem(y, 2)
    yp = y + 1 - 2 * yb

    def zdev(k, core):
        return device(x, y, lax.rem(z + k + 12, 12), core)

    def xdev(k):
        return device(lax.rem(x + k, NX), y, z, c)

    def ydev(k):
        return device(x, lax.rem(y + k, NY), z, c)

    def gdev(k):
        return device(x, y, zh * NZL + lax.rem(zl + k, NZL), c)

    other, part, partother = device(x, y, z, oc), device(x, yp, z, c), device(x, yp, z, oc)

    def remote(src, dst, ssem, rsem, dev):
        return pltpu.make_async_remote_copy(src, dst, ssem, rsem, device_id=dev, device_id_type=MESH)

    loads = [pltpu.make_async_copy(g_hbm, gv, lsem.at[0]), pltpu.make_async_copy(qt_hbm, qv, lsem.at[1]),
             pltpu.make_async_copy(e_hbm, ev, lsem.at[2])]
    for l in loads:
        l.start()

    def xload(k):
        cols = pl.ds(pl.multiple_of(lax.rem(x + k, NX) * XC, 128), XC)
        return pltpu.make_async_copy(x_hbm.at[:, cols], xv.at[:, cols], lsem.at[3 + k % 4])
    for k in (1, 2, 3, 4):
        xload(k).start()
    wcol = pl.multiple_of((c * NZL + zl) * KD, KD)
    wrow = lambda core, off=0: pl.multiple_of((yb * 2 + core) * SL + off, 64)
    wown = pltpu.make_async_copy(w_hbm.at[pl.ds(wrow(c), SL)], wbuf.at[:, pl.ds(wcol, KD)], lsem.at[7])
    wown.start()

    barrier = pltpu.get_barrier_semaphore()
    greet = ([xdev(k) for k in (1, 2, 3)] + [ydev(k) for k in range(1, 8)] + [zdev(k, c) for k in (4, -4)]
             + [gdev(k) for k in (1, 2, 3)] + [zdev(k, cc) for k in (1, -1, 2, -2) for cc in (0, 1)] + [other, partother])
    for d in greet:
        pl.semaphore_signal(barrier, inc=1, device_id=d, device_id_type=MESH)

    loads[0].wait()
    loads[1].wait()
    row = lax.broadcasted_iota(jnp.int32, (R, KD), 0)
    col = lax.broadcasted_iota(jnp.int32, (R, KD), 1)
    q0 = qv[...]
    aug[...] = jnp.where(col == row + R, 1.0, 0.0)
    aug[:, :R] = mm(q0, q0, NT, HIGH)
    a = aug[...]
    for k in range(R):
        s = lax.rsqrt(a[k:k + 1, k:k + 1])
        rn = a[k:k + 1] * s
        a = jnp.where(row == k, rn, a - jnp.where(row > k, a[:, k:k + 1] * s, 0.0) * rn)
    aug[...] = a
    qh, ql = split(mm(aug[:, R:2 * R], q0, NN, HIGH))
    q2 = jnp.concatenate([qh, ql], axis=0)
    gq = mm(q2, gv[...], NT)
    gh, gl = split(gq[:R] + gq[R:])
    g2 = jnp.concatenate([gh, gl], axis=0)

    pl.semaphore_wait(barrier, len(greet))

    gsend = [remote(gv.at[pl.ds(pl.multiple_of(lax.rem(zl + k, NZL) * 128, 128), 128)], gbuf.at[0, :, pl.ds(wcol, KD)],
                    sg.at[k - 1], dg.at[k - 1], gdev(k)) for k in (1, 2, 3)]
    for s in gsend:
        s.start()
    gbuf[0, :, pl.ds(wcol, KD)] = gv[pl.ds(pl.multiple_of(zl * 128, 128), 128)]
    loads[2].wait()

    asend = []
    for k in (2, 1, 3, 4):
        xload(k).wait()
        ch = lax.rem(x + k, NX)
        base = pl.multiple_of(ch * XC, 128)
        for off in (0, 384, 768):
            r = mm(g2, xv[:, pl.ds(base + off, 384)], NN) + mm(q2, ev[pl.ds(base + off, 384)], NT)
            if k < 4:
                ploc[ch, :, pl.ds(off, 384)] = (r[:R] + r[R:]).astype(BF16)
            else:
                pown[:, pl.ds(off, 384)] = r[:R] + r[R:]
        if k < 4:
            a = remote(ploc.at[ch], ra.at[k - 1], sa.at[k - 1], da.at[k - 1], xdev(k))
            a.start()
            asend.append(a)

    wsend = [remote(w_hbm.at[pl.ds(wrow(oc), SL)], wbuf.at[:, pl.ds(wcol, KD)], sw.at[0], dw.at[0], other)]
    for rel, core in ((0, c), (1, oc)):
        for k in (1, -1):
            i = (1 if k == 1 else 3) + rel
            wsend.append(remote(w_hbm.at[pl.ds(wrow(core), SL)], wbuf.at[:, pl.ds(wcol, KD)], sw.at[i], dw.at[i], zdev(k, core)))
    wpass = []
    for rel, core in ((0, c), (1, oc)):
        for k in (1, -1):
            i = (5 if k == 1 else 7) + rel
            blk = wbuf.at[pl.ds(0 if k == 1 else SL // 2, SL // 2),
                          pl.ds(pl.multiple_of((core * NZL + lax.rem(zl + NZL - k, NZL)) * KD, KD), KD)]
            wpass.append(remote(blk, blk, sw.at[i], dw.at[i], zdev(k, c)))
    for s in wsend[:3]:
        s.start()

    def merge(j, carry):
        rows = pl.ds(pl.multiple_of(j * 256, 256), 256)
        m = mm(xv[:, rows], gv[...], TN) + ev[rows].astype(F32)
        h, l = split(m)
        mhi[rows] = h
        mlo[rows] = l
        return carry
    lax.fori_loop(0, 18, merge, 0)
    outs = []

    def put(src, dst):
        cp = pltpu.make_async_copy(src, dst, osem.at[len(outs)])
        cp.start()
        outs.append(cp)
    put(mhi, mhi_out)
    put(mlo, mlo_out)

    for s in asend:
        s.wait_recv()
    for s in wsend[3:]:
        s.start()
    tot = pown[...] + ra[0].astype(F32) + ra[1].astype(F32) + ra[2].astype(F32)
    pa[0] = tot[:, :HALF]
    pa[1, :, pl.ds(0, XC - HALF)] = tot[:, HALF:]
    pa[1, :, pl.ds(XC - HALF, 2 * HALF - XC)] = jnp.zeros((R, 2 * HALF - XC), F32)

    def piece(ref, j):
        return ref.at[j // 4, pl.ds(pl.multiple_of(lax.rem(j, 4) * 8, 8), 8)]

    bsend = []
    for k in range(1, 8):
        b = remote(piece(pa, lax.rem(y + k, NY)), rb.at[k - 1], sb.at[k - 1], db.at[k - 1], ydev(k))
        b.start()
        bsend.append(b)

    for s in gsend:
        s.wait_recv()
    half = pl.ds(pl.multiple_of(c * 512, 512), 512)
    rsend = [remote(gbuf.at[0, :, half], gbuf.at[i, :, half], sr.at[k], dr.at[k], d)
             for k, (i, d) in enumerate([(0, other), (1, part), (1, partother)])]
    for s in rsend:
        s.start()

    for s in bsend:
        s.wait_recv()
    own = piece(pa, y)[...]
    for k in range(7):
        own = own + rb[k]
    rc[zh] = own

    csend = []
    for k, dz_ in ((0, 4), (1, -4)):
        b = remote(rc.at[zh], rc.at[zh], sc.at[k], dc.at[k], zdev(dz_, c))
        b.start()
        csend.append(b)
    for s in csend:
        s.wait_recv()
    piece(pd, y)[...] = rc[0] + rc[1] + rc[2]

    dsend = []
    for k in range(1, 8):
        b = remote(piece(pd, y), piece(pd, y), sd.at[k - 1], dd.at[k - 1], ydev(k))
        b.start()
        dsend.append(b)
    for s in wsend[1:]:
        s.wait_recv()
    for s in wpass:
        s.start()
    for s in dsend:
        s.wait_recv()

    pb[...] = pd[...].astype(BF16)
    pe[x] = pb[...]
    esend = []
    for k in (2, 1, 3):
        b = remote(pb, pe.at[x], se.at[k - 1], de.at[k - 1], xdev(k))
        b.start()
        esend.append(b)

    for s in rsend:
        s.wait_recv()
    wown.wait()
    for s in wsend[:1] + wpass:
        s.wait_recv()

    def grad(j, carry):
        rows = pl.ds(pl.multiple_of(j * 384, 128), 384)
        for b in range(2):
            igres[pl.ds(b * 128, 128), rows] = mm(gbuf[b], wbuf[rows], NT).astype(BF16)
        return carry
    lax.fori_loop(0, 3, grad, 0)
    scol = pl.ds(pl.multiple_of((yb * 2 + c) * SL, 128), SL)
    osend = []
    for k, (b, core, d) in enumerate([(0, oc, other), (1, c, part), (1, oc, partother)]):
        s = remote(igres.at[pl.ds(pl.multiple_of(b * 128 + core * 64, 64), 64)], igbuf.at[:, scol], so.at[k], do.at[k], d)
        s.start()
        osend.append(s)
    igbuf[:, scol] = igres[pl.ds(pl.multiple_of(c * 64, 64), 64)]
    def right(ch):
        tot = jnp.zeros((R, KD), F32)
        for h, n in ((0, HALF), (1, XC - HALF)):
            ph = pe[ch, h, :, :n]
            rows = pl.ds(pl.multiple_of(ch * XC + h * HALF, 128), n)
            tot = tot + mm(ph, mhi[rows], NN) + mm(ph, mlo[rows], NN)
        return tot

    qp = right(x)
    for k, s in ((1, esend[1]), (3, esend[2]), (2, esend[0])):
        s.wait_recv()
        qp = qp + right(lax.rem(x + 4 - k, NX))

    rx[x] = qp
    fsend = []
    for k in (1, 2, 3):
        b = remote(rx.at[x], rx.at[x], sx.at[k - 1], dx.at[k - 1], xdev(k))
        b.start()
        fsend.append(b)

    gram = jnp.zeros((R, R), F32)
    for ch in range(NX):
        for h, n in ((0, HALF), (1, XC - HALF)):
            b = pe[ch, h, :, :n]
            gram = gram + mm(b, b, NT)
    aug[...] = jnp.where(col == row + R, 1.0, 0.0)
    aug[:, :R] = gram

    def factor(k, carry):
        a = aug[...]
        r = jnp.sum(jnp.where(row == k, a, 0.0), axis=0, keepdims=True)
        cl = jnp.sum(jnp.where(col == k, a, 0.0), axis=1, keepdims=True)
        pivot = jnp.sum(jnp.where(col[:1] == k, r, 0.0), axis=1, keepdims=True)
        s = 1.0 / jnp.sqrt(pivot)
        rn = r * s
        aug[...] = jnp.where(row == k, rn, jnp.where(row > k, a - (cl * s) * rn, a))
        return carry

    for s in fsend:
        s.wait_recv()
    rz[zh] = rx[0] + rx[1] + rx[2] + rx[3]

    hsend = []
    for k, dz_ in ((0, 4), (1, -4)):
        b = remote(rz.at[zh], rz.at[zh], sz.at[k], dz.at[k], zdev(dz_, c))
        b.start()
        hsend.append(b)
    lax.fori_loop(0, 16, factor, 0)
    for s in hsend:
        s.wait_recv()
    ry[y] = rz[0] + rz[1] + rz[2]

    ysend = []
    for k in range(1, 8):
        b = remote(ry.at[y], ry.at[y], sy.at[k - 1], dy.at[k - 1], ydev(k))
        b.start()
        ysend.append(b)
    lax.fori_loop(16, R, factor, 0)
    linv = aug[:, R:2 * R]
    for ch in range(NX):
        for h, n in ((0, HALF), (1, XC - HALF)):
            cols = pl.ds(ch * XC + h * HALF, n)
            p = mm(linv, pe[ch, h, :, :n].astype(F32), NN, HIGH)
            pf[:, cols] = p
            ph, pl_ = split(p)
            at[cols] = jnp.concatenate([ph, pl_, ph, jnp.zeros_like(ph)], axis=0).T
    put(at, at_out)
    put(pf, pf_out)
    for s in osend:
        s.wait_recv()
    put(igbuf, ig_out)
    for s in ysend:
        s.wait_recv()
    q = ry[0]
    for k in range(1, 8):
        q = q + ry[k]
    qf[...] = mm(linv, q, NN, HIGH) * (1.0 / (NX * NY * NZH))
    put(qf, qf_out)
    for s in asend + bsend + csend + dsend + esend + fsend + hsend + ysend + wsend + wpass + gsend + rsend + osend:
        s.wait_send()
    for s in outs:
        s.wait()


def last(at_in, mhi_in, mlo_in, ig_in, pf_in, qf_in, err_out, ig_out, pt_out, qf_out, at, mhi, mlo, qf, ig, pf, err, sem, lsem):
    def load(a, b, i):
        cp = pltpu.make_async_copy(a, b, lsem.at[i])
        cp.start()
        return cp
    qload = load(qf_in, qf, 0)
    loads = []
    for h in range(3):
        part = pl.ds(h * 1536, 1536)
        loads.append([load(at_in.at[part], at.at[part], 1 + 3 * h), load(mhi_in.at[part], mhi.at[part], 2 + 3 * h),
                      load(mlo_in.at[part], mlo.at[part], 3 + 3 * h)])
    through = [(qload, qf, qf_out), (load(ig_in, ig, 10), ig, ig_out), (load(pf_in, pf, 11), pf, pt_out)]
    copies = [pltpu.make_async_copy(b, o, sem.at[i]) for i, (l, b, o) in enumerate(through)]
    qload.wait()
    copies[0].start()
    bh, bl = split(qf[...])
    b4 = jnp.concatenate([bh, bh, bl, jnp.zeros_like(bl)], axis=0)
    for h in range(3):
        for l in loads[h]:
            l.wait()

        def finish(j, carry):
            rows = pl.ds(pl.multiple_of(h * 1536 + j * 256, 256), 256)
            a = mm(at[rows], b4, NN)
            err[rows] = ((mhi[rows].astype(F32) - a) + mlo[rows].astype(F32)).astype(BF16)
            return carry
        lax.fori_loop(0, 6, finish, 0)
        part = pl.ds(h * 1536, 1536)
        c = pltpu.make_async_copy(err.at[part], err_out.at[part], sem.at[3 + h])
        c.start()
        copies.append(c)
        if h < 2:
            through[1 + h][0].wait()
            copies[1 + h].start()
    for c in copies:
        c.wait()


def shards(layer_input, key_grad, key_weight, error_state, q_start):
    dma = lambda n: pltpu.SemaphoreType.DMA((n,))
    hbm = pl.BlockSpec(memory_space=pltpu.HBM)
    shape = jax.ShapeDtypeStruct
    parts = pl.pallas_call(
        kernel,
        out_shape=(shape((D, KD), BF16), shape((D, KD), BF16), shape((D, KD), BF16),
                   shape((TOK // 8, D), BF16), shape((R, D), F32), shape((R, KD), F32)),
        in_specs=[hbm] * 5,
        out_specs=[hbm] * 6,
        scratch_shapes=[
            pltpu.VMEM((TOK, D), BF16), pltpu.VMEM((TOK, KD), BF16), pltpu.VMEM((D, KD), BF16), pltpu.VMEM((R, KD), F32),
            pltpu.VMEM((SL, 1024), BF16), pltpu.VMEM((2, 128, 1024), BF16), pltpu.VMEM((256, SL), BF16), pltpu.VMEM((64, D), BF16),
            pltpu.VMEM((NX, R, XC), BF16), pltpu.VMEM((R, XC), F32), pltpu.VMEM((3, R, XC), BF16), pltpu.VMEM((2, R, HALF), F32),
            pltpu.VMEM((7, 8, HALF), F32), pltpu.VMEM((NZH, 8, HALF), F32), pltpu.VMEM((2, R, HALF), F32), pltpu.VMEM((2, R, HALF), BF16),
            pltpu.VMEM((NX, 2, R, HALF), BF16), pltpu.VMEM((D, KD), BF16), pltpu.VMEM((D, KD), BF16),
            pltpu.VMEM((NX, R, KD), F32), pltpu.VMEM((NZH, R, KD), F32), pltpu.VMEM((NY, R, KD), F32),
            pltpu.VMEM((R, KD), F32), pltpu.VMEM((R, D), F32), pltpu.VMEM((D, KD), BF16), pltpu.VMEM((R, KD), F32),
            dma(8), dma(3), dma(3), dma(7), dma(7), dma(2), dma(2), dma(7), dma(7), dma(3), dma(3),
            dma(3), dma(3), dma(2), dma(2), dma(7), dma(7), dma(9), dma(9), dma(3), dma(3), dma(3), dma(3), dma(3), dma(3), dma(6),
        ],
        compiler_params=pltpu.CompilerParams(collective_id=0, has_side_effects=True, vmem_limit_bytes=60 << 20),
        name="powersgd",
    )(layer_input, key_grad, key_weight, error_state[0], q_start.T)
    err, ig, pt, qt = pl.pallas_call(
        last,
        out_shape=(shape((D, KD), BF16), shape((TOK // 8, D), BF16), shape((R, D), F32), shape((R, KD), F32)),
        in_specs=[hbm] * 6,
        out_specs=[hbm] * 4,
        scratch_shapes=[pltpu.VMEM((D, KD), BF16), pltpu.VMEM((D, KD), BF16), pltpu.VMEM((D, KD), BF16), pltpu.VMEM((R, KD), F32),
                        pltpu.VMEM((64, D), BF16), pltpu.VMEM((R, D), F32), pltpu.VMEM((D, KD), BF16), dma(6), dma(12)],
        compiler_params=pltpu.CompilerParams(vmem_limit_bytes=60 << 20),
        name="finish",
    )(*parts)
    return (err[None], ig, pt.T[None], qt.T)


def solution(mesh):
    return jax.shard_map(
        shards,
        mesh=mesh,
        in_specs=(
            P("dp", None),
            P("dp", "tensor"),
            P(None, "tensor"),
            P("dp", None, "tensor"),
            P("tensor", None),
        ),
        out_specs=(
            P("dp", None, "tensor"),
            P(("dp", "tensor"), None),
            P("tensor", None, None),
            P("tensor", None),
        ),
        check_vma=False,
    )
```

```python
import functools

import jax
import jax.numpy as jnp
from jax import lax
from jax.experimental import pallas as pl
from jax.experimental.pallas import tpu as pltpu
from jax.sharding import PartitionSpec as P

MESH = pl.DeviceIdType.MESH
F32, BF16 = jnp.float32, jnp.bfloat16
NX, NZH, NY, NZL, NC = 4, 3, 8, 4, 2
D, R, KD, TOK = 4608, 32, 128, 512
XC = D // NX
HALF = 640
SL = D // 4
HIGH = lax.Precision.HIGHEST
NT = (((1,), (1,)), ((), ()))
TN = (((0,), (0,)), ((), ()))
NN = (((1,), (0,)), ((), ()))


def mm(a, b, dims, precision=None):
    return lax.dot_general(a, b, dims, precision=precision, preferred_element_type=F32)


def split(a):
    hi = a.astype(BF16)
    return hi, (a - hi.astype(F32)).astype(BF16)


def device(x, y, z, c):
    return ((x * NZH + z // NZL) * NY + y, lax.rem(z, NZL) * NC + c)


def kernel(x_hbm, g_hbm, w_hbm, e_hbm, qt_hbm,
           at_out, mhi_out, mlo_out, ig_out, pf_out, qf_out,
           xv, gv, ev, qv, wbuf, gbuf, igres, igbuf,
           ploc, pown, ra, pa, rb, rc, pd, pb, pe, mhi, mlo, rx, rz, ry, aug, pf, at, qf,
           lsem, sa, da, sb, db, sc, dc, sd, dd, se, de,
           sx, dx, sz, dz, sy, dy, sw, dw, sg, dg, sr, dr, so, do, osem):
    dp, t = lax.axis_index("dp"), lax.axis_index("tensor")
    x, zh, y = dp // (NZH * NY), lax.rem(dp // NY, NZH), lax.rem(dp, NY)
    zl, c = t // NC, lax.rem(t, NC)
    z = zh * NZL + zl
    oc = 1 - c
    yb = lax.rem(y, 2)
    yp = y + 1 - 2 * yb

    def zdev(k, core):
        return device(x, y, lax.rem(z + k + 12, 12), core)

    def xdev(k):
        return device(lax.rem(x + k, NX), y, z, c)

    def ydev(k):
        return device(x, lax.rem(y + k, NY), z, c)

    def gdev(k):
        return device(x, y, zh * NZL + lax.rem(zl + k, NZL), c)

    other, part, partother = device(x, y, z, oc), device(x, yp, z, c), device(x, yp, z, oc)

    def remote(src, dst, ssem, rsem, dev):
        return pltpu.make_async_remote_copy(src, dst, ssem, rsem, device_id=dev, device_id_type=MESH)

    loads = [pltpu.make_async_copy(g_hbm, gv, lsem.at[0]), pltpu.make_async_copy(qt_hbm, qv, lsem.at[1]),
             pltpu.make_async_copy(e_hbm, ev, lsem.at[2])]
    for l in loads:
        l.start()

    def xload(k):
        cols = pl.ds(pl.multiple_of(lax.rem(x + k, NX) * XC, 128), XC)
        return pltpu.make_async_copy(x_hbm.at[:, cols], xv.at[:, cols], lsem.at[3 + k % 4])
    for k in (1, 2, 3, 4):
        xload(k).start()
    wcol = pl.multiple_of((c * NZL + zl) * KD, KD)
    wrow = lambda core, off=0: pl.multiple_of((yb * 2 + core) * SL + off, 64)
    wown = pltpu.make_async_copy(w_hbm.at[pl.ds(wrow(c), SL)], wbuf.at[:, pl.ds(wcol, KD)], lsem.at[7])
    wown.start()

    barrier = pltpu.get_barrier_semaphore()
    greet = ([xdev(k) for k in (1, 2, 3)] + [ydev(k) for k in range(1, 8)] + [zdev(k, c) for k in (4, -4)]
             + [gdev(k) for k in (1, 2, 3)] + [zdev(k, cc) for k in (1, -1, 2, -2) for cc in (0, 1)] + [other, partother])
    for d in greet:
        pl.semaphore_signal(barrier, inc=1, device_id=d, device_id_type=MESH)

    loads[0].wait()
    loads[1].wait()
    row = lax.broadcasted_iota(jnp.int32, (R, KD), 0)
    col = lax.broadcasted_iota(jnp.int32, (R, KD), 1)
    q0 = qv[...]
    aug[...] = jnp.where(col == row + R, 1.0, 0.0)
    aug[:, :R] = mm(q0, q0, NT, HIGH)
    a = aug[...]
    for k in range(R):
        s = lax.rsqrt(a[k:k + 1, k:k + 1])
        rn = a[k:k + 1] * s
        a = jnp.where(row == k, rn, a - jnp.where(row > k, a[:, k:k + 1] * s, 0.0) * rn)
    aug[...] = a
    qh, ql = split(mm(aug[:, R:2 * R], q0, NN, HIGH))
    q2 = jnp.concatenate([qh, ql], axis=0)
    gq = mm(q2, gv[...], NT)
    gh, gl = split(gq[:R] + gq[R:])
    g2 = jnp.concatenate([gh, gl], axis=0)

    pl.semaphore_wait(barrier, len(greet))

    gsend = [remote(gv.at[pl.ds(pl.multiple_of(lax.rem(zl + k, NZL) * 128, 128), 128)], gbuf.at[0, :, pl.ds(wcol, KD)],
                    sg.at[k - 1], dg.at[k - 1], gdev(k)) for k in (1, 2, 3)]
    for s in gsend:
        s.start()
    gbuf[0, :, pl.ds(wcol, KD)] = gv[pl.ds(pl.multiple_of(zl * 128, 128), 128)]
    loads[2].wait()

    asend = []
    for k in (2, 1, 3, 4):
        xload(k).wait()
        ch = lax.rem(x + k, NX)
        base = pl.multiple_of(ch * XC, 128)
        for off in (0, 384, 768):
            r = mm(g2, xv[:, pl.ds(base + off, 384)], NN) + mm(q2, ev[pl.ds(base + off, 384)], NT)
            if k < 4:
                ploc[ch, :, pl.ds(off, 384)] = (r[:R] + r[R:]).astype(BF16)
            else:
                pown[:, pl.ds(off, 384)] = r[:R] + r[R:]
        if k < 4:
            a = remote(ploc.at[ch], ra.at[k - 1], sa.at[k - 1], da.at[k - 1], xdev(k))
            a.start()
            asend.append(a)

    wsend = [remote(w_hbm.at[pl.ds(wrow(oc), SL)], wbuf.at[:, pl.ds(wcol, KD)], sw.at[0], dw.at[0], other)]
    for rel, core in ((0, c), (1, oc)):
        for k in (1, -1):
            i = (1 if k == 1 else 3) + rel
            wsend.append(remote(w_hbm.at[pl.ds(wrow(core), SL)], wbuf.at[:, pl.ds(wcol, KD)], sw.at[i], dw.at[i], zdev(k, core)))
    wpass = []
    for rel, core in ((0, c), (1, oc)):
        for k in (1, -1):
            i = (5 if k == 1 else 7) + rel
            blk = wbuf.at[pl.ds(0 if k == 1 else SL // 2, SL // 2),
                          pl.ds(pl.multiple_of((core * NZL + lax.rem(zl + NZL - k, NZL)) * KD, KD), KD)]
            wpass.append(remote(blk, blk, sw.at[i], dw.at[i], zdev(k, c)))
    for s in wsend[:3]:
        s.start()

    def merge(j, carry):
        rows = pl.ds(pl.multiple_of(j * 256, 256), 256)
        m = mm(xv[:, rows], gv[...], TN) + ev[rows].astype(F32)
        h, l = split(m)
        mhi[rows] = h
        mlo[rows] = l
        return carry
    lax.fori_loop(0, 18, merge, 0)
    outs = []

    def put(src, dst):
        cp = pltpu.make_async_copy(src, dst, osem.at[len(outs)])
        cp.start()
        outs.append(cp)
    put(mhi, mhi_out)
    put(mlo, mlo_out)

    for s in asend:
        s.wait_recv()
    for s in wsend[3:]:
        s.start()
    tot = pown[...] + ra[0].astype(F32) + ra[1].astype(F32) + ra[2].astype(F32)
    pa[0] = tot[:, :HALF]
    pa[1, :, pl.ds(0, XC - HALF)] = tot[:, HALF:]
    pa[1, :, pl.ds(XC - HALF, 2 * HALF - XC)] = jnp.zeros((R, 2 * HALF - XC), F32)

    def piece(ref, j):
        return ref.at[j // 4, pl.ds(pl.multiple_of(lax.rem(j, 4) * 8, 8), 8)]

    bsend = []
    for k in range(1, 8):
        b = remote(piece(pa, lax.rem(y + k, NY)), rb.at[k - 1], sb.at[k - 1], db.at[k - 1], ydev(k))
        b.start()
        bsend.append(b)

    for s in gsend:
        s.wait_recv()
    half = pl.ds(pl.multiple_of(c * 512, 512), 512)
    rsend = [remote(gbuf.at[0, :, half], gbuf.at[i, :, half], sr.at[k], dr.at[k], d)
             for k, (i, d) in enumerate([(0, other), (1, part), (1, partother)])]
    for s in rsend:
        s.start()

    for s in bsend:
        s.wait_recv()
    own = piece(pa, y)[...]
    for k in range(7):
        own = own + rb[k]
    rc[zh] = own

    csend = []
    for k, dz_ in ((0, 4), (1, -4)):
        b = remote(rc.at[zh], rc.at[zh], sc.at[k], dc.at[k], zdev(dz_, c))
        b.start()
        csend.append(b)
    for s in csend:
        s.wait_recv()
    piece(pd, y)[...] = rc[0] + rc[1] + rc[2]

    dsend = []
    for k in range(1, 8):
        b = remote(piece(pd, y), piece(pd, y), sd.at[k - 1], dd.at[k - 1], ydev(k))
        b.start()
        dsend.append(b)
    for s in wsend[1:]:
        s.wait_recv()
    for s in wpass:
        s.start()
    for s in dsend:
        s.wait_recv()

    pb[...] = pd[...].astype(BF16)
    pe[x] = pb[...]
    esend = []
    for k in (2, 1, 3):
        b = remote(pb, pe.at[x], se.at[k - 1], de.at[k - 1], xdev(k))
        b.start()
        esend.append(b)

    for s in rsend:
        s.wait_recv()
    wown.wait()
    for s in wsend[:1] + wpass:
        s.wait_recv()

    def grad(j, carry):
        rows = pl.ds(pl.multiple_of(j * 384, 128), 384)
        for b in range(2):
            igres[pl.ds(b * 128, 128), rows] = mm(gbuf[b], wbuf[rows], NT).astype(BF16)
        return carry
    lax.fori_loop(0, 3, grad, 0)
    scol = pl.ds(pl.multiple_of((yb * 2 + c) * SL, 128), SL)
    osend = []
    for k, (b, core, d) in enumerate([(0, oc, other), (1, c, part), (1, oc, partother)]):
        s = remote(igres.at[pl.ds(pl.multiple_of(b * 128 + core * 64, 64), 64)], igbuf.at[:, scol], so.at[k], do.at[k], d)
        s.start()
        osend.append(s)
    igbuf[:, scol] = igres[pl.ds(pl.multiple_of(c * 64, 64), 64)]
    def right(ch):
        tot = jnp.zeros((R, KD), F32)
        for h, n in ((0, HALF), (1, XC - HALF)):
            ph = pe[ch, h, :, :n]
            rows = pl.ds(pl.multiple_of(ch * XC + h * HALF, 128), n)
            tot = tot + mm(ph, mhi[rows], NN) + mm(ph, mlo[rows], NN)
        return tot

    qp = right(x)
    for k, s in ((1, esend[1]), (3, esend[2]), (2, esend[0])):
        s.wait_recv()
        qp = qp + right(lax.rem(x + 4 - k, NX))

    rx[x] = qp
    fsend = []
    for k in (1, 2, 3):
        b = remote(rx.at[x], rx.at[x], sx.at[k - 1], dx.at[k - 1], xdev(k))
        b.start()
        fsend.append(b)

    gram = jnp.zeros((R, R), F32)
    for ch in range(NX):
        for h, n in ((0, HALF), (1, XC - HALF)):
            b = pe[ch, h, :, :n]
            gram = gram + mm(b, b, NT)
    aug[...] = jnp.where(col == row + R, 1.0, 0.0)
    aug[:, :R] = gram

    def factor(k, carry):
        a = aug[...]
        r = jnp.sum(jnp.where(row == k, a, 0.0), axis=0, keepdims=True)
        cl = jnp.sum(jnp.where(col == k, a, 0.0), axis=1, keepdims=True)
        pivot = jnp.sum(jnp.where(col[:1] == k, r, 0.0), axis=1, keepdims=True)
        s = 1.0 / jnp.sqrt(pivot)
        rn = r * s
        aug[...] = jnp.where(row == k, rn, jnp.where(row > k, a - (cl * s) * rn, a))
        return carry

    for s in fsend:
        s.wait_recv()
    rz[zh] = rx[0] + rx[1] + rx[2] + rx[3]

    hsend = []
    for k, dz_ in ((0, 4), (1, -4)):
        b = remote(rz.at[zh], rz.at[zh], sz.at[k], dz.at[k], zdev(dz_, c))
        b.start()
        hsend.append(b)
    lax.fori_loop(0, 16, factor, 0)
    for s in hsend:
        s.wait_recv()
    ry[y] = rz[0] + rz[1] + rz[2]

    ysend = []
    for k in range(1, 8):
        b = remote(ry.at[y], ry.at[y], sy.at[k - 1], dy.at[k - 1], ydev(k))
        b.start()
        ysend.append(b)
    lax.fori_loop(16, R, factor, 0)
    linv = aug[:, R:2 * R]
    for ch in range(NX):
        for h, n in ((0, HALF), (1, XC - HALF)):
            cols = pl.ds(ch * XC + h * HALF, n)
            p = mm(linv, pe[ch, h, :, :n].astype(F32), NN, HIGH)
            pf[:, cols] = p
            ph, pl_ = split(p)
            at[cols] = jnp.concatenate([ph, pl_, ph, jnp.zeros_like(ph)], axis=0).T
    put(at, at_out)
    put(pf, pf_out)
    for s in osend:
        s.wait_recv()
    put(igbuf, ig_out)
    for s in ysend:
        s.wait_recv()
    q = ry[0]
    for k in range(1, 8):
        q = q + ry[k]
    qf[...] = mm(linv, q, NN, HIGH) * (1.0 / (NX * NY * NZH))
    put(qf, qf_out)
    for s in asend + bsend + csend + dsend + esend + fsend + hsend + ysend + wsend + wpass + gsend + rsend + osend:
        s.wait_send()
    for s in outs:
        s.wait()


def last(at_in, mhi_in, mlo_in, ig_in, pf_in, qf_in, err_out, ig_out, pt_out, qf_out, at, mhi, mlo, qf, ig, pf, err, sem, lsem):
    def load(a, b, i):
        cp = pltpu.make_async_copy(a, b, lsem.at[i])
        cp.start()
        return cp
    qload = load(qf_in, qf, 0)
    loads = []
    for h in range(3):
        part = pl.ds(h * 1536, 1536)
        loads.append([load(at_in.at[part], at.at[part], 1 + 3 * h), load(mhi_in.at[part], mhi.at[part], 2 + 3 * h),
                      load(mlo_in.at[part], mlo.at[part], 3 + 3 * h)])
    through = [(qload, qf, qf_out), (load(ig_in, ig, 10), ig, ig_out), (load(pf_in, pf, 11), pf, pt_out)]
    copies = [pltpu.make_async_copy(b, o, sem.at[i]) for i, (l, b, o) in enumerate(through)]
    qload.wait()
    copies[0].start()
    bh, bl = split(qf[...])
    b4 = jnp.concatenate([bh, bh, bl, jnp.zeros_like(bl)], axis=0)
    for h in range(3):
        for l in loads[h]:
            l.wait()

        part = pl.ds(h * 1536, 1536)
        a = mm(at[part], b4, NN)
        err[part] = ((mhi[part].astype(F32) - a) + mlo[part].astype(F32)).astype(BF16)
        c = pltpu.make_async_copy(err.at[part], err_out.at[part], sem.at[3 + h])
        c.start()
        copies.append(c)
        if h < 2:
            through[1 + h][0].wait()
            copies[1 + h].start()
    for c in copies:
        c.wait()


def shards(layer_input, key_grad, key_weight, error_state, q_start):
    dma = lambda n: pltpu.SemaphoreType.DMA((n,))
    hbm = pl.BlockSpec(memory_space=pltpu.HBM)
    shape = jax.ShapeDtypeStruct
    parts = pl.pallas_call(
        kernel,
        out_shape=(shape((D, KD), BF16), shape((D, KD), BF16), shape((D, KD), BF16),
                   shape((TOK // 8, D), BF16), shape((R, D), F32), shape((R, KD), F32)),
        in_specs=[hbm] * 5,
        out_specs=[hbm] * 6,
        scratch_shapes=[
            pltpu.VMEM((TOK, D), BF16), pltpu.VMEM((TOK, KD), BF16), pltpu.VMEM((D, KD), BF16), pltpu.VMEM((R, KD), F32),
            pltpu.VMEM((SL, 1024), BF16), pltpu.VMEM((2, 128, 1024), BF16), pltpu.VMEM((256, SL), BF16), pltpu.VMEM((64, D), BF16),
            pltpu.VMEM((NX, R, XC), BF16), pltpu.VMEM((R, XC), F32), pltpu.VMEM((3, R, XC), BF16), pltpu.VMEM((2, R, HALF), F32),
            pltpu.VMEM((7, 8, HALF), F32), pltpu.VMEM((NZH, 8, HALF), F32), pltpu.VMEM((2, R, HALF), F32), pltpu.VMEM((2, R, HALF), BF16),
            pltpu.VMEM((NX, 2, R, HALF), BF16), pltpu.VMEM((D, KD), BF16), pltpu.VMEM((D, KD), BF16),
            pltpu.VMEM((NX, R, KD), F32), pltpu.VMEM((NZH, R, KD), F32), pltpu.VMEM((NY, R, KD), F32),
            pltpu.VMEM((R, KD), F32), pltpu.VMEM((R, D), F32), pltpu.VMEM((D, KD), BF16), pltpu.VMEM((R, KD), F32),
            dma(8), dma(3), dma(3), dma(7), dma(7), dma(2), dma(2), dma(7), dma(7), dma(3), dma(3),
            dma(3), dma(3), dma(2), dma(2), dma(7), dma(7), dma(9), dma(9), dma(3), dma(3), dma(3), dma(3), dma(3), dma(3), dma(6),
        ],
        compiler_params=pltpu.CompilerParams(collective_id=0, has_side_effects=True, vmem_limit_bytes=60 << 20),
        name="powersgd",
    )(layer_input, key_grad, key_weight, error_state[0], q_start.T)
    err, ig, pt, qt = pl.pallas_call(
        last,
        out_shape=(shape((D, KD), BF16), shape((TOK // 8, D), BF16), shape((R, D), F32), shape((R, KD), F32)),
        in_specs=[hbm] * 6,
        out_specs=[hbm] * 4,
        scratch_shapes=[pltpu.VMEM((D, KD), BF16), pltpu.VMEM((D, KD), BF16), pltpu.VMEM((D, KD), BF16), pltpu.VMEM((R, KD), F32),
                        pltpu.VMEM((64, D), BF16), pltpu.VMEM((R, D), F32), pltpu.VMEM((D, KD), BF16), dma(6), dma(12)],
        compiler_params=pltpu.CompilerParams(vmem_limit_bytes=60 << 20),
        name="finish",
    )(*parts)
    return (err[None], ig, pt.T[None], qt.T)


def solution(mesh):
    return jax.shard_map(
        shards,
        mesh=mesh,
        in_specs=(
            P("dp", None),
            P("dp", "tensor"),
            P(None, "tensor"),
            P("dp", None, "tensor"),
            P("tensor", None),
        ),
        out_specs=(
            P("dp", None, "tensor"),
            P(("dp", "tensor"), None),
            P("tensor", None, None),
            P("tensor", None),
        ),
        check_vma=False,
    )
```

```python
import functools

import jax
import jax.numpy as jnp
from jax import lax
from jax.experimental import pallas as pl
from jax.experimental.pallas import tpu as pltpu
from jax.sharding import PartitionSpec as P

MESH = pl.DeviceIdType.MESH
F32, BF16 = jnp.float32, jnp.bfloat16
NX, NZH, NY, NZL, NC = 4, 3, 8, 4, 2
D, R, KD, TOK = 4608, 32, 128, 512
XC = D // NX
HALF = 640
SL = D // 4
HIGH = lax.Precision.HIGHEST
NT = (((1,), (1,)), ((), ()))
TN = (((0,), (0,)), ((), ()))
NN = (((1,), (0,)), ((), ()))


def mm(a, b, dims, precision=None):
    return lax.dot_general(a, b, dims, precision=precision, preferred_element_type=F32)


def split(a):
    hi = a.astype(BF16)
    return hi, (a - hi.astype(F32)).astype(BF16)


def factor(a):
    row = lax.broadcasted_iota(jnp.int32, (R, KD), 0)
    for k in range(R):
        s = 1.0 / jnp.sqrt(a[k:k + 1, k:k + 1])
        rn = a[k:k + 1] * s
        a = jnp.where(row == k, rn, a - jnp.where(row > k, a[:, k:k + 1] * s, 0.0) * rn)
    return a


def device(x, y, z, c):
    return ((x * NZH + z // NZL) * NY + y, lax.rem(z, NZL) * NC + c)


def kernel(x_hbm, g_hbm, w_hbm, e_hbm, qt_hbm,
           at_out, mhi_out, mlo_out, ig_out, pf_out, qf_out,
           xv, gv, ev, qv, wbuf, gbuf, igres, igbuf,
           ploc, pown, ra, pa, rb, rc, pd, pb, pe, mhi, mlo, rx, rz, ry, aug, pf, at, qf,
           lsem, sa, da, sb, db, sc, dc, sd, dd, se, de,
           sx, dx, sz, dz, sy, dy, sw, dw, sg, dg, sr, dr, so, do, osem):
    dp, t = lax.axis_index("dp"), lax.axis_index("tensor")
    x, zh, y = dp // (NZH * NY), lax.rem(dp // NY, NZH), lax.rem(dp, NY)
    zl, c = t // NC, lax.rem(t, NC)
    z = zh * NZL + zl
    oc = 1 - c
    yb = lax.rem(y, 2)
    yp = y + 1 - 2 * yb

    def zdev(k, core):
        return device(x, y, lax.rem(z + k + 12, 12), core)

    def xdev(k):
        return device(lax.rem(x + k, NX), y, z, c)

    def ydev(k):
        return device(x, lax.rem(y + k, NY), z, c)

    def gdev(k):
        return device(x, y, zh * NZL + lax.rem(zl + k, NZL), c)

    other, part, partother = device(x, y, z, oc), device(x, yp, z, c), device(x, yp, z, oc)

    def remote(src, dst, ssem, rsem, dev):
        return pltpu.make_async_remote_copy(src, dst, ssem, rsem, device_id=dev, device_id_type=MESH)

    loads = [pltpu.make_async_copy(g_hbm, gv, lsem.at[0]), pltpu.make_async_copy(qt_hbm, qv, lsem.at[1]),
             pltpu.make_async_copy(e_hbm, ev, lsem.at[2])]
    for l in loads:
        l.start()

    def xload(k):
        cols = pl.ds(pl.multiple_of(lax.rem(x + k, NX) * XC, 128), XC)
        return pltpu.make_async_copy(x_hbm.at[:, cols], xv.at[:, cols], lsem.at[3 + k % 4])
    for k in (1, 2, 3, 4):
        xload(k).start()
    wcol = pl.multiple_of((c * NZL + zl) * KD, KD)
    wrow = lambda core, off=0: pl.multiple_of((yb * 2 + core) * SL + off, 64)
    wown = pltpu.make_async_copy(w_hbm.at[pl.ds(wrow(c), SL)], wbuf.at[:, pl.ds(wcol, KD)], lsem.at[7])
    wown.start()

    barrier = pltpu.get_barrier_semaphore()
    greet = ([xdev(k) for k in (1, 2, 3)] + [ydev(k) for k in range(1, 8)] + [zdev(k, c) for k in (4, -4)]
             + [gdev(k) for k in (1, 2, 3)] + [zdev(k, cc) for k in (1, -1, 2, -2) for cc in (0, 1)] + [other, partother])
    for d in greet:
        pl.semaphore_signal(barrier, inc=1, device_id=d, device_id_type=MESH)

    loads[0].wait()
    loads[1].wait()
    row = lax.broadcasted_iota(jnp.int32, (R, KD), 0)
    col = lax.broadcasted_iota(jnp.int32, (R, KD), 1)
    q0 = qv[...]
    aug[...] = jnp.where(col == row + R, 1.0, 0.0)
    aug[:, :R] = mm(q0, q0, NT, HIGH)
    aug[...] = factor(aug[...])
    qh, ql = split(mm(aug[:, R:2 * R], q0, NN, HIGH))
    q2 = jnp.concatenate([qh, ql], axis=0)
    gq = mm(q2, gv[...], NT)
    gh, gl = split(gq[:R] + gq[R:])
    g2 = jnp.concatenate([gh, gl], axis=0)

    pl.semaphore_wait(barrier, len(greet))

    gsend = [remote(gv.at[pl.ds(pl.multiple_of(lax.rem(zl + k, NZL) * 128, 128), 128)], gbuf.at[0, :, pl.ds(wcol, KD)],
                    sg.at[k - 1], dg.at[k - 1], gdev(k)) for k in (1, 2, 3)]
    for s in gsend:
        s.start()
    gbuf[0, :, pl.ds(wcol, KD)] = gv[pl.ds(pl.multiple_of(zl * 128, 128), 128)]
    loads[2].wait()

    asend = []
    for k in (2, 1, 3, 4):
        xload(k).wait()
        ch = lax.rem(x + k, NX)
        base = pl.multiple_of(ch * XC, 128)
        for off in (0, 384, 768):
            r = mm(g2, xv[:, pl.ds(base + off, 384)], NN) + mm(q2, ev[pl.ds(base + off, 384)], NT)
            if k < 4:
                ploc[ch, :, pl.ds(off, 384)] = (r[:R] + r[R:]).astype(BF16)
            else:
                pown[:, pl.ds(off, 384)] = r[:R] + r[R:]
        if k < 4:
            a = remote(ploc.at[ch], ra.at[k - 1], sa.at[k - 1], da.at[k - 1], xdev(k))
            a.start()
            asend.append(a)

    wsend = [remote(w_hbm.at[pl.ds(wrow(oc), SL)], wbuf.at[:, pl.ds(wcol, KD)], sw.at[0], dw.at[0], other)]
    for rel, core in ((0, c), (1, oc)):
        for k in (1, -1):
            i = (1 if k == 1 else 3) + rel
            wsend.append(remote(w_hbm.at[pl.ds(wrow(core), SL)], wbuf.at[:, pl.ds(wcol, KD)], sw.at[i], dw.at[i], zdev(k, core)))
    wpass = []
    for rel, core in ((0, c), (1, oc)):
        for k in (1, -1):
            i = (5 if k == 1 else 7) + rel
            blk = wbuf.at[pl.ds(0 if k == 1 else SL // 2, SL // 2),
                          pl.ds(pl.multiple_of((core * NZL + lax.rem(zl + NZL - k, NZL)) * KD, KD), KD)]
            wpass.append(remote(blk, blk, sw.at[i], dw.at[i], zdev(k, c)))
    for s in wsend[:3]:
        s.start()

    def merge(j, carry):
        rows = pl.ds(pl.multiple_of(j * 256, 256), 256)
        m = mm(xv[:, rows], gv[...], TN) + ev[rows].astype(F32)
        h, l = split(m)
        mhi[rows] = h
        mlo[rows] = l
        return carry
    outs = []

    def put(src, dst):
        cp = pltpu.make_async_copy(src, dst, osem.at[len(outs)])
        cp.start()
        outs.append(cp)

    for s in asend:
        s.wait_recv()
    for s in wsend[3:]:
        s.start()
    tot = pown[...] + ra[0].astype(F32) + ra[1].astype(F32) + ra[2].astype(F32)
    pa[0] = tot[:, :HALF]
    pa[1, :, pl.ds(0, XC - HALF)] = tot[:, HALF:]
    pa[1, :, pl.ds(XC - HALF, 2 * HALF - XC)] = jnp.zeros((R, 2 * HALF - XC), F32)

    def piece(ref, j):
        return ref.at[j // 4, pl.ds(pl.multiple_of(lax.rem(j, 4) * 8, 8), 8)]

    bsend = []
    for k in (4, 3, 5, 2, 6, 1, 7):
        b = remote(piece(pa, lax.rem(y + k, NY)), rb.at[k - 1], sb.at[k - 1], db.at[k - 1], ydev(k))
        b.start()
        bsend.append(b)

    for s in gsend:
        s.wait_recv()
    half = pl.ds(pl.multiple_of(c * 512, 512), 512)
    rsend = [remote(gbuf.at[0, :, half], gbuf.at[i, :, half], sr.at[k], dr.at[k], d)
             for k, (i, d) in enumerate([(0, other), (1, part), (1, partother)])]
    for s in rsend:
        s.start()

    lax.fori_loop(0, 9, merge, 0)
    for s in bsend:
        s.wait_recv()
    own = piece(pa, y)[...]
    for k in range(7):
        own = own + rb[k]
    rc[zh] = own

    csend = []
    for k, dz_ in ((0, 4), (1, -4)):
        b = remote(rc.at[zh], rc.at[zh], sc.at[k], dc.at[k], zdev(dz_, c))
        b.start()
        csend.append(b)
    lax.fori_loop(9, 18, merge, 0)
    put(mhi, mhi_out)
    put(mlo, mlo_out)
    for s in csend:
        s.wait_recv()
    piece(pd, y)[...] = rc[0] + rc[1] + rc[2]

    dsend = []
    for k in (4, 3, 5, 2, 6, 1, 7):
        b = remote(piece(pd, y), piece(pd, y), sd.at[k - 1], dd.at[k - 1], ydev(k))
        b.start()
        dsend.append(b)
    for s in wsend[1:]:
        s.wait_recv()
    for s in wpass:
        s.start()
    for s in dsend:
        s.wait_recv()

    pb[...] = pd[...].astype(BF16)
    pe[x] = pb[...]
    esend = []
    for k in (2, 1, 3):
        b = remote(pb, pe.at[x], se.at[k - 1], de.at[k - 1], xdev(k))
        b.start()
        esend.append(b)

    for s in rsend:
        s.wait_recv()
    wown.wait()
    for s in wsend[:1] + wpass:
        s.wait_recv()

    def grad(j, carry):
        rows = pl.ds(pl.multiple_of(j * 384, 128), 384)
        for b in range(2):
            igres[pl.ds(b * 128, 128), rows] = mm(gbuf[b], wbuf[rows], NT).astype(BF16)
        return carry
    lax.fori_loop(0, 3, grad, 0)
    scol = pl.ds(pl.multiple_of((yb * 2 + c) * SL, 128), SL)
    osend = []
    for k, (b, core, d) in enumerate([(0, oc, other), (1, c, part), (1, oc, partother)]):
        s = remote(igres.at[pl.ds(pl.multiple_of(b * 128 + core * 64, 64), 64)], igbuf.at[:, scol], so.at[k], do.at[k], d)
        s.start()
        osend.append(s)
    igbuf[:, scol] = igres[pl.ds(pl.multiple_of(c * 64, 64), 64)]
    def right(ch):
        tot = jnp.zeros((R, KD), F32)
        for h, n in ((0, HALF), (1, XC - HALF)):
            ph = pe[ch, h, :, :n]
            rows = pl.ds(pl.multiple_of(ch * XC + h * HALF, 128), n)
            tot = tot + mm(ph, mhi[rows], NN) + mm(ph, mlo[rows], NN)
        return tot

    qp = right(x)
    for k, s in ((1, esend[1]), (3, esend[2]), (2, esend[0])):
        s.wait_recv()
        qp = qp + right(lax.rem(x + 4 - k, NX))

    rx[x] = qp
    fsend = []
    for k in (1, 2, 3):
        b = remote(rx.at[x], rx.at[x], sx.at[k - 1], dx.at[k - 1], xdev(k))
        b.start()
        fsend.append(b)

    gram = jnp.zeros((R, R), F32)
    for ch in range(NX):
        for h, n in ((0, HALF), (1, XC - HALF)):
            b = pe[ch, h, :, :n]
            gram = gram + mm(b, b, NT)
    aug[...] = jnp.where(col == row + R, 1.0, 0.0)
    aug[:, :R] = gram

    aug[...] = factor(aug[...])
    linv = aug[:, R:2 * R]
    for s in fsend:
        s.wait_recv()
    rz[zh] = rx[0] + rx[1] + rx[2] + rx[3]

    hsend = []
    for k, dz_ in ((0, 4), (1, -4)):
        b = remote(rz.at[zh], rz.at[zh], sz.at[k], dz.at[k], zdev(dz_, c))
        b.start()
        hsend.append(b)
    for ch in range(NX):
        for h, n in ((0, HALF), (1, XC - HALF)):
            cols = pl.ds(ch * XC + h * HALF, n)
            p = mm(linv, pe[ch, h, :, :n].astype(F32), NN, HIGH)
            pf[:, cols] = p
            ph, pl_ = split(p)
            at[cols] = jnp.concatenate([ph, pl_, ph, jnp.zeros_like(ph)], axis=0).T
    put(at, at_out)
    put(pf, pf_out)
    for s in hsend:
        s.wait_recv()
    ry[y] = rz[0] + rz[1] + rz[2]

    ysend = []
    for k in (4, 3, 5, 2, 6, 1, 7):
        b = remote(ry.at[y], ry.at[y], sy.at[k - 1], dy.at[k - 1], ydev(k))
        b.start()
        ysend.append(b)
    for s in osend:
        s.wait_recv()
    put(igbuf, ig_out)
    for s in ysend:
        s.wait_recv()
    q = ry[0]
    for k in range(1, 8):
        q = q + ry[k]
    qf[...] = mm(linv, q, NN, HIGH) * (1.0 / (NX * NY * NZH))
    put(qf, qf_out)
    for s in asend + bsend + csend + dsend + esend + fsend + hsend + ysend + wsend + wpass + gsend + rsend + osend:
        s.wait_send()
    for s in outs:
        s.wait()


def last(at_in, mhi_in, mlo_in, ig_in, pf_in, qf_in, err_out, ig_out, pt_out, qf_out, at, mhi, mlo, qf, ig, pf, err, sem, lsem):
    def load(a, b, i):
        cp = pltpu.make_async_copy(a, b, lsem.at[i])
        cp.start()
        return cp
    qload = load(qf_in, qf, 0)
    loads = []
    for h in range(3):
        part = pl.ds(h * 1536, 1536)
        loads.append([load(at_in.at[part], at.at[part], 1 + 3 * h), load(mhi_in.at[part], mhi.at[part], 2 + 3 * h),
                      load(mlo_in.at[part], mlo.at[part], 3 + 3 * h)])
    through = [(qload, qf, qf_out), (load(ig_in, ig, 10), ig, ig_out), (load(pf_in, pf, 11), pf, pt_out)]
    copies = [pltpu.make_async_copy(b, o, sem.at[i]) for i, (l, b, o) in enumerate(through)]
    qload.wait()
    copies[0].start()
    bh, bl = split(qf[...])
    b4 = jnp.concatenate([bh, bh, bl, jnp.zeros_like(bl)], axis=0)
    for h in range(3):
        for l in loads[h]:
            l.wait()

        part = pl.ds(h * 1536, 1536)
        a = mm(at[part], b4, NN)
        err[part] = ((mhi[part].astype(F32) - a) + mlo[part].astype(F32)).astype(BF16)
        c = pltpu.make_async_copy(err.at[part], err_out.at[part], sem.at[3 + h])
        c.start()
        copies.append(c)
        if h < 2:
            through[1 + h][0].wait()
            copies[1 + h].start()
    for c in copies:
        c.wait()


def shards(layer_input, key_grad, key_weight, error_state, q_start):
    dma = lambda n: pltpu.SemaphoreType.DMA((n,))
    hbm = pl.BlockSpec(memory_space=pltpu.HBM)
    shape = jax.ShapeDtypeStruct
    parts = pl.pallas_call(
        kernel,
        out_shape=(shape((D, KD), BF16), shape((D, KD), BF16), shape((D, KD), BF16),
                   shape((TOK // 8, D), BF16), shape((R, D), F32), shape((R, KD), F32)),
        in_specs=[hbm] * 5,
        out_specs=[hbm] * 6,
        scratch_shapes=[
            pltpu.VMEM((TOK, D), BF16), pltpu.VMEM((TOK, KD), BF16), pltpu.VMEM((D, KD), BF16), pltpu.VMEM((R, KD), F32),
            pltpu.VMEM((SL, 1024), BF16), pltpu.VMEM((2, 128, 1024), BF16), pltpu.VMEM((256, SL), BF16), pltpu.VMEM((64, D), BF16),
            pltpu.VMEM((NX, R, XC), BF16), pltpu.VMEM((R, XC), F32), pltpu.VMEM((3, R, XC), BF16), pltpu.VMEM((2, R, HALF), F32),
            pltpu.VMEM((7, 8, HALF), F32), pltpu.VMEM((NZH, 8, HALF), F32), pltpu.VMEM((2, R, HALF), F32), pltpu.VMEM((2, R, HALF), BF16),
            pltpu.VMEM((NX, 2, R, HALF), BF16), pltpu.VMEM((D, KD), BF16), pltpu.VMEM((D, KD), BF16),
            pltpu.VMEM((NX, R, KD), F32), pltpu.VMEM((NZH, R, KD), F32), pltpu.VMEM((NY, R, KD), F32),
            pltpu.VMEM((R, KD), F32), pltpu.VMEM((R, D), F32), pltpu.VMEM((D, KD), BF16), pltpu.VMEM((R, KD), F32),
            dma(8), dma(3), dma(3), dma(7), dma(7), dma(2), dma(2), dma(7), dma(7), dma(3), dma(3),
            dma(3), dma(3), dma(2), dma(2), dma(7), dma(7), dma(9), dma(9), dma(3), dma(3), dma(3), dma(3), dma(3), dma(3), dma(6),
        ],
        compiler_params=pltpu.CompilerParams(collective_id=0, has_side_effects=True, vmem_limit_bytes=60 << 20),
        name="powersgd",
    )(layer_input, key_grad, key_weight, error_state[0], q_start.T)
    err, ig, pt, qt = pl.pallas_call(
        last,
        out_shape=(shape((D, KD), BF16), shape((TOK // 8, D), BF16), shape((R, D), F32), shape((R, KD), F32)),
        in_specs=[hbm] * 6,
        out_specs=[hbm] * 4,
        scratch_shapes=[pltpu.VMEM((D, KD), BF16), pltpu.VMEM((D, KD), BF16), pltpu.VMEM((D, KD), BF16), pltpu.VMEM((R, KD), F32),
                        pltpu.VMEM((64, D), BF16), pltpu.VMEM((R, D), F32), pltpu.VMEM((D, KD), BF16), dma(6), dma(12)],
        compiler_params=pltpu.CompilerParams(vmem_limit_bytes=60 << 20),
        name="finish",
    )(*parts)
    return (err[None], ig, pt.T[None], qt.T)


def solution(mesh):
    return jax.shard_map(
        shards,
        mesh=mesh,
        in_specs=(
            P("dp", None),
            P("dp", "tensor"),
            P(None, "tensor"),
            P("dp", None, "tensor"),
            P("tensor", None),
        ),
        out_specs=(
            P("dp", None, "tensor"),
            P(("dp", "tensor"), None),
            P("tensor", None, None),
            P("tensor", None),
        ),
        check_vma=False,
    )
```
